128 devices in a mesh: expert: 32 (over z, x, core), mp: 4 (over y).
Axes of the slice: x: 4, y: 4, z: 4, core: 2. Of those that a mesh axis runs over, the one named last changes fastest.
Arguments:
- tokens: bfloat16 [16384, 1024], P(('expert', 'mp')), may hold values from -6 to 6
- out_grad: bfloat16 [16384, 1024], P(('expert', 'mp')), may hold values from -6 to 6
- routes: int32 [16384, 8], P('expert'), may hold values from 0 to 63, all different within a row; in each aligned block of 512 rows (0 to 511, 512 to 1023, ...) at most 80 rows name the same one
- gates: float32 [16384, 8], P('expert'), may hold values from 0.05 to 0.4
- w_gate: bfloat16 [64, 1024, 1024], P('expert', None, 'mp'), may hold values from -0.1875 to 0.1875
- w_up: bfloat16 [64, 1024, 1024], P('expert', None, 'mp'), may hold values from -0.1875 to 0.1875
- w_down: bfloat16 [64, 1024, 1024], P('expert', 'mp'), may hold values from -0.1875 to 0.1875
Outputs:
- grad_tokens: bfloat16 [16384, 1024], P(('expert', 'mp'))
- grad_gate: float32 [64, 1024, 1024], P('expert', None, 'mp')
- grad_up: float32 [64, 1024, 1024], P('expert', None, 'mp')
- grad_down: float32 [64, 1024, 1024], P('expert', 'mp')
The draws below stay inside these ranges and needn't reach their ends.
Inputs may be any that keep to these rules, and one draw needn't show every extreme that they name: `routes`: each row names 8 different experts. Within each aligned block of 512 rows (the rows of one index of expert) no expert is named by more than 80 rows, a bound that some block reaches.
All inputs are finite; a program needn't handle non-finite values.
Results may differ from the reference program's by a relative error of at most 0.017.
Values may be sent and summed in bfloat16 or wider, within the bound.
A program may use at most 192 MiB of HBM per device.

```python
import math
import jax
import jax.numpy as jnp
import numpy as np
from jax import lax

D = 1024
FF = 1024
TOPK = 8
EXPERTS = 64
GROUP_TOK = 512
TOKENS = 16384
CAP = 80
FF_SLICE = 256
N_EXPERT = 32
N_MP = 4


def levels(rng, shape, cuts, low, top_value):
    factor_of = 1.0
    for axis_at, shards_of in cuts:
        draws = jax.random.uniform(jax.random.fold_in(jax.random.fold_in(rng, 6), axis_at), (shards_of,), jnp.float32, low / len(cuts), top_value / len(cuts))
        factor_of = factor_of * jnp.repeat(jnp.exp(draws), shape[axis_at] // shards_of).reshape((-1,) + (1,) * (len(shape) - 1 - axis_at))
    return factor_of


def routed_block(own_key, own, number, rows, number_of, top, most, lean):
    order = jax.random.permutation(own_key, number_of)
    packed, usual = portions_of(number_of, rows * top, most, lean, True), portions_of(number_of, rows * top, most, lean, False)
    places = jnp.arange(number_of)

    def named(lengths, offset_by):
        used = int((lengths > 0).sum())
        fixed = max(1, used // 4)
        passed = fixed + (places - fixed + offset_by * (used - fixed)) % max(1, number_of - fixed)
        return jnp.zeros((number_of,), jnp.int32).at[order[jnp.where(places < fixed, places, passed)]].set(jnp.asarray(lengths, jnp.int32))

    lengths = jnp.where(number % 4 == 0, named(packed, number // 4), named(usual, number - number // 4 - 1))
    mixed = jax.random.permutation(jax.random.fold_in(own, 3), number_of)
    giver, taker = mixed[0:number_of // 2 * 2:2], mixed[1:number_of // 2 * 2:2]
    slack = jnp.minimum(lengths[giver] - 1, most - lengths[taker]) // 2
    slack = jnp.where((giver == order[0]) | (taker == order[0]) | (lengths[taker] == 0), 0, jnp.maximum(slack, 0))
    passed = jax.random.randint(jax.random.fold_in(own, 4), (number_of // 2,), 0, 1 << 20) % (slack + 1)
    lengths = lengths.at[giver].add(-passed).at[taker].add(passed)
    members = jnp.searchsorted(jnp.cumsum(lengths), jnp.arange(rows * top), side="right").astype(jnp.int32)
    grid = members.reshape(top, rows).T
    grid = grid[jax.random.permutation(jax.random.fold_in(own, 1), rows)]
    offset_by = jax.random.randint(jax.random.fold_in(own, 2), (rows, 1), 0, top)
    return jnp.take_along_axis(grid, (jnp.arange(top)[None, :] + offset_by) % top, axis=1)


def portions_of(count, total, bound, skew, full):
    weights = [(1 << 20) // math.isqrt(grade ** skew) + 1 for grade in range(1, count + 1)]
    largest = bound if full else min(bound, max(-(-total // count), total * weights[0] // sum(weights)))
    least = 1 if total - largest >= count - 1 else 0
    counts, spare = [largest] + [least] * (count - 1), total - largest - least * (count - 1)
    while spare > 0:
        free = [i for i in range(1, count) if counts[i] < largest] or [i for i in range(1, count) if counts[i] < bound]
        pool, budget = sum([weights[i] for i in free]), spare
        for i in free:
            more = min(bound - counts[i], max(1, budget * weights[i] // pool), spare)
            counts[i] = counts[i] + more
            spare = spare - more
    return np.array(counts)


def gaussian(own_key, shape, width, limit, split=(), held_as=jnp.bfloat16):
    gain = levels(own_key, shape, split, -0.22, 0.18) if split else 1.0
    values = jax.random.normal(own_key, shape, jnp.float32) * width * gain
    return jnp.minimum(jnp.maximum(values, -limit), limit).astype(held_as)


def setup_inputs(seed: int = 0) -> dict:
    streams_of = jax.random.split(jax.random.key(seed), 8)
    tokens = gaussian(streams_of[0], (TOKENS, D), 1.0, 6.0, ((0, 128),))
    out_grad = gaussian(streams_of[1], (TOKENS, D), 1.0, 6.0, ((0, 128),))
    routes_keys = jax.random.split(jax.random.fold_in(streams_of[2], 1), TOKENS // GROUP_TOK)
    routes_turns = jax.random.permutation(jax.random.fold_in(streams_of[2], 3), TOKENS // GROUP_TOK)
    routes = jax.vmap(lambda own, number: routed_block(jax.random.fold_in(streams_of[2], 2), own, number, GROUP_TOK, EXPERTS, TOPK, CAP, 1))(routes_keys, routes_turns).reshape((TOKENS, TOPK))
    gates = jnp.clip(0.05 + 0.35 * jax.random.uniform(streams_of[3], (TOKENS, TOPK), jnp.float32) ** levels(streams_of[3], (TOKENS, TOPK), ((0, 32),), -0.2, 0.2), 0.05, 0.4)
    w_gate = gaussian(streams_of[4], (EXPERTS, D, FF), D ** -0.5, 0.1875, ((0, 32), (2, 4)))
    w_up = gaussian(streams_of[5], (EXPERTS, D, FF), D ** -0.5, 0.1875, ((0, 32), (2, 4)))
    w_down = gaussian(streams_of[6], (EXPERTS, FF, D), FF ** -0.5, 0.1875, ((0, 32), (1, 4)))
    return dict(tokens=tokens, out_grad=out_grad, routes=routes, gates=gates, w_gate=w_gate, w_up=w_up, w_down=w_down)


def reference(tokens, out_grad, routes, gates, w_gate, w_up, w_down):
    route_total = TOKENS * TOPK
    blocks = TOKENS // GROUP_TOK
    per_expert = N_EXPERT * CAP
    flat = routes.reshape(blocks, GROUP_TOK * TOPK)
    expert_ids = jnp.arange(EXPERTS, dtype=jnp.int32)
    onehot = (flat[:, :, None] == expert_ids[None, None, :]).astype(jnp.int32)
    before = jnp.sum((jnp.cumsum(onehot, axis=1) - onehot) * onehot, axis=2)
    block_ids = jnp.arange(blocks, dtype=jnp.int32)[:, None]
    where = (flat * per_expert + block_ids * CAP + before).reshape(-1)
    route_ids = jnp.arange(route_total, dtype=jnp.int32)
    owner = jnp.full((EXPERTS * per_expert,), route_total, jnp.int32).at[where].set(route_ids)
    owner = owner.reshape(EXPERTS, per_expert)
    x_pad = jnp.concatenate([tokens, jnp.zeros((1, D), jnp.bfloat16)], axis=0)
    dy_pad = jnp.concatenate([out_grad, jnp.zeros((1, D), jnp.bfloat16)], axis=0)
    gate_pad = jnp.concatenate([gates.reshape(-1), jnp.zeros((1,), jnp.float32)], axis=0)

    def one_expert(carry, pieces):
        owner_rows, wgate, wup, wdown = pieces
        token_rows = (owner_rows // TOPK).astype(jnp.int32)
        x_rows = x_pad[token_rows]
        scaled = (gate_pad[owner_rows][:, None] * dy_pad[token_rows].astype(jnp.float32)).astype(jnp.bfloat16)
        pre_gate = jnp.dot(x_rows, wgate, preferred_element_type=jnp.float32)
        pre_up = jnp.dot(x_rows, wup, preferred_element_type=jnp.float32)
        sig = jax.nn.sigmoid(pre_gate)
        hidden = (pre_gate * sig * pre_up).astype(jnp.bfloat16)
        d_hidden = jnp.dot(scaled, wdown.T, preferred_element_type=jnp.float32)
        grad_down = jnp.dot(hidden.T, scaled, preferred_element_type=jnp.float32)
        d_up = (d_hidden * pre_gate * sig).astype(jnp.bfloat16)
        d_gate = (d_hidden * pre_up * sig * (1.0 + pre_gate * (1.0 - sig))).astype(jnp.bfloat16)
        grad_gate = jnp.dot(x_rows.T, d_gate, preferred_element_type=jnp.float32)
        grad_up = jnp.dot(x_rows.T, d_up, preferred_element_type=jnp.float32)
        dg_blocks = d_gate.astype(jnp.float32).reshape(-1, N_MP, FF_SLICE)
        du_blocks = d_up.astype(jnp.float32).reshape(-1, N_MP, FF_SLICE)
        wg_blocks = wgate.astype(jnp.float32).reshape(D, N_MP, FF_SLICE)
        wu_blocks = wup.astype(jnp.float32).reshape(D, N_MP, FF_SLICE)
        part = jnp.einsum('mqf,dqf->mqd', dg_blocks, wg_blocks) + jnp.einsum('mqf,dqf->mqd', du_blocks, wu_blocks)
        part = part.astype(jnp.bfloat16).astype(jnp.float32)
        carry = carry.at[token_rows].add(jnp.sum(part, axis=1))
        return carry, (grad_gate, grad_up, grad_down)

    start = jnp.zeros((TOKENS + 1, D), jnp.float32)
    total, grads = lax.scan(one_expert, start, (owner, w_gate, w_up, w_down))
    grad_tokens = total[:TOKENS].astype(jnp.bfloat16)
    return grad_tokens, grads[0], grads[1], grads[2]
```

```python
import jax
import jax.numpy as jnp
from jax import lax
from jax.experimental import pallas as pl
from jax.experimental.pallas import tpu as pltpu
from jax.sharding import PartitionSpec as P

MESH = pl.DeviceIdType.MESH
BF16, F32 = jnp.bfloat16, jnp.float32
TOK, TILES, LANES = 128, 8, 128
CAP = 80
META = TILES * 2 * TOK
MROWS = META + 32
SPLIT = ((0, 688), (688, 688), (1376, 704))
BACK = ((0, 336), (336, 336), (672, 352))
ORDER = ((0, 1, 2), (1, 2, 0), (2, 0, 1))


def where_am_i():
    e = lax.axis_index("expert")
    return (e // 8, (e // 2) % 4, lax.axis_index("mp")), e % 2


def dev_of(pos, core):
    return ((pos[0] * 4 + pos[1]) * 2 + core, pos[2])


def index_of(pos, core):
    return ((pos[0] * 4 + pos[1]) * 2 + core) * 4 + pos[2]


def lin(pos):
    return (pos[0] * 4 + pos[1]) * 4 + pos[2]


def moved(pos, axis, by):
    p = list(pos)
    p[axis] = (p[axis] + by + 4) % 4
    return tuple(p)


def rows_of(split, r, half):
    start, size = split[r]
    low = (size // 32) * 16
    if half is None:
        return start, size
    return (start, low) if half == 0 else (start + low, size - low)


def greet(me, core):
    barrier = pltpu.get_barrier_semaphore()
    for axis in range(3):
        for d in (1, -1):
            pl.semaphore_signal(barrier, inc=1, device_id=dev_of(moved(me, axis, d), core), device_id_type=MESH)
    pl.semaphore_signal(barrier, inc=1, device_id=dev_of(me, 1 - core), device_id_type=MESH)
    pl.semaphore_wait(barrier, 7)


def gather_kernel(msg, buf, send_sem, recv_sem, pair_send, pair_recv, own_sem):
    me, core = where_am_i()
    other = dev_of(me, 1 - core)
    greet(me, core)
    own = pltpu.make_async_copy(msg, buf.at[index_of(me, core)], own_sem)
    own.start()

    def ring(r, pos, half, axis, d, mine=False):
        start, size = rows_of(SPLIT, r, half)
        idx = index_of(pos, core)
        src = msg if mine else buf.at[idx]
        return pltpu.make_async_remote_copy(
            src_ref=src.at[pl.ds(start, size)], dst_ref=buf.at[idx, pl.ds(start, size)],
            send_sem=send_sem, recv_sem=recv_sem.at[r, lin(pos), 0 if half is None else half],
            device_id=dev_of(moved(me, axis, d), core), device_id_type=MESH)

    def pair(r, pos, mine=False):
        start, size = SPLIT[r]
        idx = index_of(pos, core)
        src = msg if mine else buf.at[idx]
        pltpu.make_async_remote_copy(
            src_ref=src.at[pl.ds(start, size)], dst_ref=buf.at[idx, pl.ds(start, size)],
            send_sem=pair_send, recv_sem=pair_recv,
            device_id=other, device_id_type=MESH).start()

    def send_full(r, pos, phase, mine=False):
        for p in range(phase, 3):
            for d in (1, -1):
                ring(r, pos, None, ORDER[r][p], d, mine).start()

    def near(r, base, phase):
        axis = ORDER[r][phase]
        for d in (1, -1):
            pos = moved(base, axis, -d)
            ring(r, pos, None, axis, d).wait_recv()
            ring(r, pos, 0 if d == 1 else 1, axis, d).start()
            pair(r, pos)
            send_full(r, pos, phase + 1)

    def far(r, base, phase):
        axis = ORDER[r][phase]
        pos = moved(base, axis, 2)
        for half in (0, 1):
            ring(r, pos, half, axis, 1).wait_recv()
        pair(r, pos)
        send_full(r, pos, phase + 1)

    for r in range(3):
        send_full(r, me, 0, mine=True)
    for r in range(3):
        pair(r, me, mine=True)
    for step in (near, far):
        for r in range(3):
            step(r, me, 0)
    for step in (near, far):
        def line(i, c, step=step):
            for r in range(3):
                step(r, moved(me, ORDER[r][0], i), 1)
            return c
        lax.fori_loop(0, 4, line, 0)
    for step in (near, far):
        def plane(i, c, step=step):
            for r in range(3):
                step(r, moved(moved(me, ORDER[r][0], i // 4), ORDER[r][1], i % 4), 2)
            return c
        lax.fori_loop(0, 16, plane, 0)
    own.wait()
    half = buf.at[pl.ds(0, 64)]
    pltpu.make_async_copy(half, half, pair_recv).wait()
    pltpu.make_async_copy(half, half, pair_send).wait()
    most = buf.at[pl.ds(0, 63)]
    pltpu.make_async_copy(most, most, send_sem).wait()


def gather_all(msg):
    dma = pltpu.SemaphoreType.DMA
    return pl.pallas_call(
        gather_kernel,
        out_shape=jax.ShapeDtypeStruct((128, MROWS, LANES), BF16),
        in_specs=[pl.BlockSpec(memory_space=pl.ANY)],
        out_specs=pl.BlockSpec(memory_space=pl.ANY),
        scratch_shapes=[dma, dma((3, 64, 2)), dma, dma, dma],
        compiler_params=pltpu.CompilerParams(collective_id=0, has_side_effects=True),
    )(msg)


def tn(a, b):
    return lax.dot_general(a, b, (((0,), (0,)), ((), ())), preferred_element_type=F32)


def nt(a, b):
    return lax.dot_general(a, b, (((1,), (1,)), ((), ())), preferred_element_type=F32)


BLOCKS = 4


def expert_kernel(buf, wg, wu, wd, partial, gg, gu, gd, xs, ss, ps, part):
    step = pl.program_id(0)
    first = lax.axis_index("expert") * 2

    @pl.when(step == 0)
    def _():
        gg[...] = jnp.zeros_like(gg)
        gu[...] = jnp.zeros_like(gu)
        gd[...] = jnp.zeros_like(gd)

    slots = lax.broadcasted_iota(jnp.int32, (CAP, TOK), 0).astype(F32)

    def pick(b, c):
        hots, gates = [[], []], [0.0, 0.0]
        for y in range(4):
            meta = buf[b * 4 + y, pl.ds(META, 32), :].astype(F32)
            for j in range(2):
                named = (meta[0:8] == (first + j).astype(F32)).astype(F32)
                at = jnp.sum(named * (meta[8:16] + 1.0), axis=0, keepdims=True) - 1.0
                gate = jnp.sum(named * (meta[16:24] + meta[24:32]), axis=0, keepdims=True)
                hot = (slots == at).astype(F32)
                hots[j].append(hot)
                gates[j] = gates[j] + jnp.sum(hot * gate, axis=1, keepdims=True)
        hot = jnp.concatenate([jnp.concatenate(h, axis=1) for h in hots], axis=0).astype(BF16)
        gate = jnp.concatenate(gates, axis=0)
        ps[b] = hot
        for t in range(0, TILES, 2):
            def cols(at):
                return jnp.concatenate([
                    jnp.concatenate([buf[b * 4 + y, pl.ds((t + u) * 2 * TOK + at, TOK), :] for u in range(2)], axis=1)
                    for y in range(4)], axis=0)
            x = jnp.dot(hot, cols(0), preferred_element_type=F32).astype(BF16)
            s = (gate * jnp.dot(hot, cols(TOK), preferred_element_type=F32)).astype(BF16)
            for j in range(2):
                rows = pl.ds(pl.multiple_of(b * CAP, 16), CAP)
                xs[j, rows, pl.ds(t * LANES, 2 * LANES)] = x[j * CAP:(j + 1) * CAP]
                ss[j, rows, pl.ds(t * LANES, 2 * LANES)] = s[j * CAP:(j + 1) * CAP]
        return c

    lax.fori_loop(0, BLOCKS, pick, 0)
    for j in range(2):
        x, s = xs[j], ss[j]
        pre_gate = jnp.dot(x, wg[j], preferred_element_type=F32)
        pre_up = jnp.dot(x, wu[j], preferred_element_type=F32)
        d_hidden = nt(s, wd[j])
        sig = jax.nn.sigmoid(pre_gate)
        act = pre_gate * sig
        hidden = (act * pre_up).astype(BF16)
        d_up = (d_hidden * act).astype(BF16)
        d_gate = (d_hidden * pre_up * sig * (1.0 + pre_gate * (1.0 - sig))).astype(BF16)
        gd[j] += tn(hidden, s)
        gg[j] += tn(x, d_gate)
        gu[j] += tn(x, d_up)
        part[j] = (nt(d_gate, wg[j]) + nt(d_up, wu[j])).astype(BF16)

    def place(b, c):
        hot = ps[b]
        rows = pl.ds(pl.multiple_of(b * CAP, 16), CAP)
        for t in range(0, TILES, 2):
            both = jnp.concatenate([part[j, rows, pl.ds(t * LANES, 2 * LANES)] for j in range(2)], axis=0)
            out = tn(hot, both).astype(BF16)
            for y in range(4):
                for u in range(2):
                    partial[b * 4 + y, pl.ds((t + u) * TOK, TOK), :] = out[y * TOK:(y + 1) * TOK, u * LANES:(u + 1) * LANES]
        return c

    lax.fori_loop(0, BLOCKS, place, 0)


def experts(buf, wg, wu, wd):
    whole = lambda a: pl.BlockSpec(a.shape, lambda i: (0, 0, 0), pipeline_mode=pl.Buffered(1))
    g = jax.ShapeDtypeStruct(wg.shape, F32)
    d = jax.ShapeDtypeStruct(wd.shape, F32)
    n = BLOCKS * 4
    return pl.pallas_call(
        expert_kernel,
        grid=(128 // n,),
        out_shape=(jax.ShapeDtypeStruct((128, TILES * TOK, LANES), BF16), g, g, d),
        in_specs=[pl.BlockSpec((n, MROWS, LANES), lambda i: (i, 0, 0)), whole(wg), whole(wu), whole(wd)],
        out_specs=(pl.BlockSpec((n, TILES * TOK, LANES), lambda i: (i, 0, 0)), whole(g), whole(g), whole(d)),
        scratch_shapes=[pltpu.VMEM((2, BLOCKS * CAP, 1024), BF16), pltpu.VMEM((2, BLOCKS * CAP, 1024), BF16),
                        pltpu.VMEM((BLOCKS, 2 * CAP, 512), BF16), pltpu.VMEM((2, BLOCKS * CAP, 1024), BF16)],
        compiler_params=pltpu.CompilerParams(vmem_limit_bytes=60 * 1024 * 1024),
    )(buf, wg, wu, wd)


def scatter_kernel(partial, out, mine, theirs, land, send_sem, recv_sem, pair_send, pair_recv, load_sem, out_sem):
    me, core = where_am_i()
    other = dev_of(me, 1 - core)
    greet(me, core)

    def pair(r, pos):
        start, size = BACK[r]
        return pltpu.make_async_remote_copy(
            src_ref=partial.at[index_of(pos, 1 - core), pl.ds(start, size)],
            dst_ref=theirs.at[lin(pos), pl.ds(start, size)],
            send_sem=pair_send, recv_sem=pair_recv.at[r, lin(pos)],
            device_id=other, device_id_type=MESH)

    def load(r, pos, kind):
        start, size = BACK[r]
        return pltpu.make_async_copy(
            partial.at[index_of(pos, core), pl.ds(start, size)], mine.at[lin(pos), pl.ds(start, size)],
            load_sem.at[kind])

    def prepare(r, pos):
        pair(r, pos).wait_recv()
        start, size = BACK[r]
        rows = pl.ds(start, size)
        mine[lin(pos), rows, :] = mine[lin(pos), rows, :] + theirs[lin(pos), rows, :]

    def slot(r, pos, phase):
        a = [pos[k] for k in ORDER[r]]
        return (20, 16 + a[0], a[0] * 4 + a[1])[phase]

    def hop(r, pos, phase, kind, d):
        half = None if kind else (0 if d == 1 else 1)
        start, size = rows_of(BACK, r, half)
        s = slot(r, pos, phase)
        lane = 2 if kind == 0 else (0 if d == 1 else 1)
        sem = (0 if d == 1 else 1) + 2 * kind
        return pltpu.make_async_remote_copy(
            src_ref=mine.at[lin(pos), pl.ds(start, size)],
            dst_ref=land.at[r, s * 3 + lane, pl.ds(start - BACK[r][0], size)],
            send_sem=send_sem, recv_sem=recv_sem.at[r, s, sem],
            device_id=dev_of(moved(me, ORDER[r][phase], d), core), device_id_type=MESH)

    def add(r, pos, phase, kind, d):
        hop(r, pos, phase, kind, d).wait_recv()
        half = None if kind else (0 if d == 1 else 1)
        start, size = rows_of(BACK, r, half)
        lane = 2 if kind == 0 else (0 if d == 1 else 1)
        rows = pl.ds(start, size)
        mine[lin(pos), rows, :] = (mine[lin(pos), rows, :]
                                   + land[r, slot(r, pos, phase) * 3 + lane, pl.ds(start - BACK[r][0], size), :])

    def far(r, base, phase):
        pos = moved(base, ORDER[r][phase], 2)
        if phase == 2:
            prepare(r, pos)
        for d in (1, -1):
            hop(r, pos, phase, 0, d).start()

    def near(r, base, phase):
        for d in (1, -1):
            pos = moved(base, ORDER[r][phase], d)
            if phase == 2:
                prepare(r, pos)
            add(r, pos, phase, 0, d)
            hop(r, pos, phase, 1, d).start()

    def here(r, base, phase):
        if phase == 2:
            prepare(r, base)
        for d in (1, -1):
            add(r, base, phase, 1, d)

    def order(i):
        return 2 + i

    def plane_base(r, i):
        return moved(moved(me, ORDER[r][0], order(i // 4)), ORDER[r][1], order(i % 4))

    def fetch(kind, offsets):
        def body(i, c):
            for r in range(3):
                for o in offsets:
                    pos = moved(plane_base(r, i), ORDER[r][2], o)
                    pair(r, pos).start()
                    load(r, pos, kind).start()
            return c
        return body

    for kind, offsets in enumerate(((2,), (1, -1), (0,))):
        lax.fori_loop(0, 16, fetch(kind, offsets), 0)
    for kind, step in enumerate((far, near, here)):
        loaded = mine.at[pl.ds(0, (16, 32, 16)[kind])]
        pltpu.make_async_copy(loaded, loaded, load_sem.at[kind]).wait()

        def plane(i, c, step=step):
            for r in range(3):
                step(r, plane_base(r, i), 2)
            return c
        lax.fori_loop(0, 16, plane, 0)
    for step in (far, near, here):
        def line(i, c, step=step):
            for r in range(3):
                step(r, moved(me, ORDER[r][0], order(i)), 1)
            return c
        lax.fori_loop(0, 4, line, 0)
    for step in (far, near, here):
        for r in range(3):
            step(r, me, 0)
    done = pltpu.make_async_copy(mine.at[lin(me)], out, out_sem)
    done.start()
    done.wait()
    pltpu.make_async_copy(theirs, theirs, pair_send).wait()
    most = theirs.at[pl.ds(0, 63)]
    pltpu.make_async_copy(most, most, send_sem).wait()


def scatter_all(partial):
    dma = pltpu.SemaphoreType.DMA
    rows = TILES * TOK
    return pl.pallas_call(
        scatter_kernel,
        out_shape=jax.ShapeDtypeStruct((rows, LANES), BF16),
        in_specs=[pl.BlockSpec(memory_space=pl.ANY)],
        out_specs=pl.BlockSpec(memory_space=pl.ANY),
        scratch_shapes=[pltpu.VMEM((64, rows, LANES), BF16), pltpu.VMEM((64, rows, LANES), BF16),
                        pltpu.VMEM((3, 63, 352, LANES), BF16),
                        dma, dma((3, 21, 4)), dma, dma((3, 64)), dma((3,)), dma],
        compiler_params=pltpu.CompilerParams(collective_id=1, has_side_effects=True, vmem_limit_bytes=60 * 1024 * 1024),
    )(partial)


def shards(tokens, out_grad, routes, gates, w_gate, w_up, w_down):
    y = lax.axis_index("mp")
    ids = jnp.arange(64, dtype=jnp.int32)
    named = jnp.sum((routes[:, :, None] == ids).astype(F32), axis=1)
    below = jnp.tril(jnp.ones((512, 512), F32), -1)
    before = jnp.dot(below.astype(BF16), named.astype(BF16), preferred_element_type=F32)
    before = jnp.sum(jnp.where(routes[:, :, None] == ids, before[:, None, :], 0.0), axis=2)
    own = lambda a: lax.dynamic_slice_in_dim(a, y * TOK, TOK, axis=0).T
    gate = own(gates)
    high = lax.reduce_precision(gate, 8, 7)
    meta = jnp.concatenate([own(routes).astype(F32), own(before), high, gate - high], axis=0).astype(BF16)
    tiled = lambda a: a.reshape(TOK, TILES, LANES).transpose(1, 0, 2)
    msg = jnp.concatenate([tiled(tokens), tiled(out_grad)], axis=1).reshape(META, LANES)
    msg = jnp.concatenate([msg, meta], axis=0)
    buf = gather_all(msg)
    partial, grad_gate, grad_up, grad_down = experts(buf, w_gate, w_up, w_down)
    back = scatter_all(partial)
    grad_tokens = back.reshape(TILES, TOK, LANES).transpose(1, 0, 2).reshape(TOK, TILES * LANES)
    return grad_tokens, grad_gate, grad_up, grad_down


def solution(mesh):
    in_specs = (
        P(("expert", "mp"), None),
        P(("expert", "mp"), None),
        P("expert", None),
        P("expert", None),
        P("expert", None, "mp"),
        P("expert", None, "mp"),
        P("expert", "mp", None),
    )
    out_specs = (
        P(("expert", "mp"), None),
        P("expert", None, "mp"),
        P("expert", None, "mp"),
        P("expert", "mp", None),
    )
    return jax.shard_map(shards, mesh=mesh, in_specs=in_specs, out_specs=out_specs, check_vma=False)
```

```python
import jax
import jax.numpy as jnp
from jax import lax
from jax.experimental import pallas as pl
from jax.experimental.pallas import tpu as pltpu
from jax.sharding import PartitionSpec as P

MESH = pl.DeviceIdType.MESH
BF16, F32 = jnp.bfloat16, jnp.float32
TOK, TILES, LANES = 128, 8, 128
CAP = 80
META = TILES * 2 * TOK
MROWS = META + 32
SPLIT = ((0, 688), (688, 688), (1376, 704))
BACK = ((0, 336), (336, 336), (672, 352))
ORDER = ((0, 1, 2), (1, 2, 0), (2, 0, 1))


def where_am_i():
    e = lax.axis_index("expert")
    return (e // 8, (e // 2) % 4, lax.axis_index("mp")), e % 2


def dev_of(pos, core):
    return ((pos[0] * 4 + pos[1]) * 2 + core, pos[2])


def index_of(pos, core):
    return ((pos[0] * 4 + pos[1]) * 2 + core) * 4 + pos[2]


def lin(pos):
    return (pos[0] * 4 + pos[1]) * 4 + pos[2]


def moved(pos, axis, by):
    p = list(pos)
    p[axis] = (p[axis] + by + 4) % 4
    return tuple(p)


def rows_of(split, r, half):
    start, size = split[r]
    low = (size // 32) * 16
    if half is None:
        return start, size
    return (start, low) if half == 0 else (start + low, size - low)


def greet(me, core):
    barrier = pltpu.get_barrier_semaphore()
    for axis in range(3):
        for d in (1, -1):
            pl.semaphore_signal(barrier, inc=1, device_id=dev_of(moved(me, axis, d), core), device_id_type=MESH)
    pl.semaphore_signal(barrier, inc=1, device_id=dev_of(me, 1 - core), device_id_type=MESH)
    pl.semaphore_wait(barrier, 7)


def tn(a, b):
    return lax.dot_general(a, b, (((0,), (0,)), ((), ())), preferred_element_type=F32)


def nt(a, b):
    return lax.dot_general(a, b, (((1,), (1,)), ((), ())), preferred_element_type=F32)


BLOCKS = 4
NEAR4 = (0, 1, 3, 2)
COL_Z = (0, 1, 3, 0, 0, 1, 3, 1, 3, 2, 0, 2, 1, 2, 3, 2)
COL_X = (0, 0, 0, 1, 3, 1, 1, 3, 3, 0, 2, 1, 2, 3, 2, 2)
AHEAD = 4
LOOK = 4


def entry(table, i):
    out = 0
    for k, v in enumerate(table):
        if v:
            out = out + jnp.where(i == k, v, 0)
    return out


def gather_kernel(msg, wg, wu, wd, buf, kept, given, gg, gu, gd, slab, xs, ss, ps, part, stage,
                  send_sem, recv_sem, pair_send, pair_recv, own_sem, load_sem, stage_sem, given_sem):
    me, core = where_am_i()
    other = dev_of(me, 1 - core)
    first = lax.axis_index("expert") * 2
    greet(me, core)
    own = pltpu.make_async_copy(msg, buf.at[index_of(me, core)], own_sem)
    own.start()

    def ring(r, pos, half, axis, d, mine=False):
        start, size = rows_of(SPLIT, r, half)
        idx = index_of(pos, core)
        src = msg if mine else buf.at[idx]
        return pltpu.make_async_remote_copy(
            src_ref=src.at[pl.ds(start, size)], dst_ref=buf.at[idx, pl.ds(start, size)],
            send_sem=send_sem, recv_sem=recv_sem.at[r, lin(pos), 0 if half is None else half],
            device_id=dev_of(moved(me, axis, d), core), device_id_type=MESH)

    def pair(r, pos, mine=False):
        start, size = SPLIT[r]
        idx = index_of(pos, core)
        src = msg if mine else buf.at[idx]
        pltpu.make_async_remote_copy(
            src_ref=src.at[pl.ds(start, size)], dst_ref=buf.at[idx, pl.ds(start, size)],
            send_sem=pair_send, recv_sem=pair_recv.at[pos[0] * 4 + pos[1]],
            device_id=other, device_id_type=MESH).start()

    def send_full(r, pos, phases, mine=False):
        for p in phases:
            for d in (1, -1):
                ring(r, pos, None, ORDER[r][p], d, mine).start()

    def forward(r, base, phase):
        axis = ORDER[r][phase]
        for d in (1, -1):
            ring(r, moved(base, axis, -d), 0 if d == 1 else 1, axis, d).start()

    def near(r, base, phase, later=(), onward=True):
        axis = ORDER[r][phase]
        for d in (1, -1):
            pos = moved(base, axis, -d)
            ring(r, pos, None, axis, d).wait_recv()
            if onward:
                ring(r, pos, 0 if d == 1 else 1, axis, d).start()
            pair(r, pos)
            send_full(r, pos, later)

    def far(r, base, phase, later=()):
        axis = ORDER[r][phase]
        pos = moved(base, axis, 2)
        for half in (0, 1):
            ring(r, pos, half, axis, 1).wait_recv()
        pair(r, pos)
        send_full(r, pos, later)

    def column(i):
        return moved(moved(me, 0, entry(COL_Z, i)), 1, entry(COL_X, i))

    def base_of(r, i):
        return moved(moved(me, 1 if r == 1 else 0, entry(NEAR4, i // 4)), 2, entry(NEAR4, i % 4))

    def issue(u):
        def whole():
            for r in (1, 2):
                send_full(r, base_of(r, u), (2,))

        def halves():
            for r in (1, 2):
                for k in range(2):
                    forward(r, base_of(r, 2 * (u - 16) + k), 2)
        if isinstance(u, int):
            whole()
        else:
            pl.when(u < 16)(whole)
            pl.when((u >= 16) & (u < 24))(halves)

    for r in range(3):
        send_full(r, me, (0, 1, 2), mine=True)
    for r in range(3):
        pair(r, me, mine=True)
    for r in range(3):
        near(r, me, 0, (1,))
    for r in range(3):
        far(r, me, 0, (1,))
    for i in (1, 2):
        send_full(0, column(i), (2,))

    def line(step):
        def body(i, c):
            for r in range(3):
                step(r, moved(me, ORDER[r][0], entry(NEAR4, i)), 1)
            return c
        return body
    lax.fori_loop(0, 4, line(near), 0)
    for u in (1, 2):
        issue(u)
    lax.fori_loop(0, 4, line(far), 0)

    gg[...] = jnp.zeros_like(gg)
    gu[...] = jnp.zeros_like(gu)
    gd[...] = jnp.zeros_like(gd)
    own.wait()

    for u in range(3, LOOK):
        issue(u)
    send_full(0, column(3), (2,))

    def along_y(i):
        near(0, column(i), 2)

        @pl.when(i + AHEAD < 16)
        def _():
            send_full(0, column(i + AHEAD), (2,))

    def unit(u):
        @pl.when(u < 16)
        def _():
            for r in (1, 2):
                near(r, base_of(r, u), 2, onward=False)

        @pl.when((u >= 16) & (u < 24))
        def _():
            for r in (1, 2):
                for k in range(2):
                    far(r, base_of(r, 2 * (u - 16) + k), 2)
        issue(u + LOOK)

    def start_up(i, c):
        unit(i)
        along_y(i)
        return c
    lax.fori_loop(0, 3, start_up, 0)

    slots = lax.broadcasted_iota(jnp.int32, (CAP, TOK), 0).astype(F32)

    def staged(k, at):
        to = pl.ds(pl.multiple_of(at * 4, 4), 4)
        mine = stage.at[pl.ds(pl.multiple_of(k * 8 + core * 4, 4), 4)]
        theirs = stage.at[pl.ds(pl.multiple_of(k * 8 + (1 - core) * 4, 4), 4)]
        return (pltpu.make_async_copy(mine, kept.at[to], stage_sem.at[k, 0]),
                pltpu.make_async_remote_copy(src_ref=theirs, dst_ref=given.at[to], send_sem=stage_sem.at[k, 1],
                                             recv_sem=given_sem, device_id=other, device_id_type=MESH))

    def stage_wait():
        for k in range(2):
            stay, go = staged(k, 0)
            stay.wait()
            go.wait_send()

    def pick(b, at):
        hots, gates = [[], []], [0.0, 0.0]
        for y in range(4):
            meta = slab[at + b * 4 + y, pl.ds(META, 32), :].astype(F32)
            for j in range(2):
                named = (meta[0:8] == (first + j).astype(F32)).astype(F32)
                where = jnp.sum(named * (meta[8:16] + 1.0), axis=0, keepdims=True) - 1.0
                gate = jnp.sum(named * (meta[16:24] + meta[24:32]), axis=0, keepdims=True)
                hot = (slots == where).astype(F32)
                hots[j].append(hot)
                gates[j] = gates[j] + jnp.sum(hot * gate, axis=1, keepdims=True)
        hot = jnp.concatenate([jnp.concatenate(h, axis=1) for h in hots], axis=0).astype(BF16)
        gate = jnp.concatenate(gates, axis=0)
        ps[b] = hot
        for t in range(0, TILES, 2):
            def cols(off):
                return jnp.concatenate([
                    jnp.concatenate([slab[at + b * 4 + y, pl.ds((t + u) * 2 * TOK + off, TOK), :] for u in range(2)], axis=1)
                    for y in range(4)], axis=0)
            x = jnp.dot(hot, cols(0), preferred_element_type=F32).astype(BF16)
            s = (gate * jnp.dot(hot, cols(TOK), preferred_element_type=F32)).astype(BF16)
            for j in range(2):
                rows = pl.ds(pl.multiple_of(b * CAP, 16), CAP)
                xs[j, rows, pl.ds(t * LANES, 2 * LANES)] = x[j * CAP:(j + 1) * CAP]
                ss[j, rows, pl.ds(t * LANES, 2 * LANES)] = s[j * CAP:(j + 1) * CAP]
        return at

    def place(b, c):
        hot = ps[b]
        rows = pl.ds(pl.multiple_of(b * CAP, 16), CAP)
        for t in range(0, TILES, 2):
            both = jnp.concatenate([part[j, rows, pl.ds(t * LANES, 2 * LANES)] for j in range(2)], axis=0)
            out = tn(hot, both).astype(BF16)
            for y in range(4):
                for u in range(2):
                    stage[b * 4 + y, pl.ds((t + u) * TOK, TOK), :] = out[y * TOK:(y + 1) * TOK, u * LANES:(u + 1) * LANES]
        return c

    def main(j):
        x, s = xs[j], ss[j]
        pre_gate = jnp.dot(x, wg[j], preferred_element_type=F32)
        pre_up = jnp.dot(x, wu[j], preferred_element_type=F32)
        d_hidden = nt(s, wd[j])
        sig = jax.nn.sigmoid(pre_gate)
        act = pre_gate * sig
        hidden = (act * pre_up).astype(BF16)
        d_up = (d_hidden * act).astype(BF16)
        d_gate = (d_hidden * pre_up * sig * (1.0 + pre_gate * (1.0 - sig))).astype(BF16)
        gd[j] += tn(hidden, s)
        gg[j] += tn(x, d_gate)
        gu[j] += tn(x, d_up)
        part[j] = (nt(d_gate, wg[j]) + nt(d_up, wu[j])).astype(BF16)

    def column_at(i):
        pos = column(i)
        return pos[0] * 4 + pos[1]

    def load(p, k):
        at = column_at(2 * p + k) * 8
        half = p % 2
        return pltpu.make_async_copy(buf.at[pl.ds(pl.multiple_of(at, 8), 8)],
                                     slab.at[pl.ds(pl.multiple_of(half * 16 + k * 8, 8), 8)], load_sem.at[half, k])

    def compute(p, c):
        live, ready = p < 8, p >= 1
        at = ((p + 1) % 2) * 16
        unit(3 * p + 3)

        @pl.when(ready)
        def _():
            load(p - 1, 0).wait()
            lax.fori_loop(0, 2, pick, at)

        @pl.when(p < 7)
        def _():
            along_y(2 * p + 3)
        unit(3 * p + 4)

        @pl.when(ready)
        def _():
            load(p - 1, 1).wait()
            lax.fori_loop(2, 4, pick, at)

        @pl.when(p < 6)
        def _():
            along_y(2 * p + 4)
        unit(3 * p + 5)

        @pl.when(ready)
        def _():
            main(0)

        @pl.when(live)
        def _():
            for k in range(2):
                far(0, column(2 * p + k), 2)

        @pl.when(ready)
        def _():
            main(1)

        @pl.when(live)
        def _():
            for k in range(2):
                zx = column_at(2 * p + k)
                theirs = buf.at[pl.ds(pl.multiple_of(zx * 8 + (1 - core) * 4, 4), 4)]
                pltpu.make_async_copy(theirs, theirs, pair_recv.at[zx]).wait()
                load(p, k).start()

        pl.when(p >= 2)(stage_wait)

        @pl.when(ready)
        def _():
            lax.fori_loop(0, BLOCKS, place, 0)
            for k in range(2):
                stay, go = staged(k, column_at(2 * (p - 1) + k))
                stay.start()
                go.start()
        return c

    lax.fori_loop(0, 9, compute, 0)
    stage_wait()
    pltpu.make_async_copy(given, given, given_sem).wait()
    half = buf.at[pl.ds(0, 64)]
    pltpu.make_async_copy(half, half, pair_send).wait()
    most = buf.at[pl.ds(0, 63)]
    pltpu.make_async_copy(most, most, send_sem).wait()


def gather_and_compute(msg, wg, wu, wd):
    dma = pltpu.SemaphoreType.DMA
    hbm, vmem = pl.BlockSpec(memory_space=pl.ANY), pl.BlockSpec(memory_space=pltpu.VMEM)
    g = jax.ShapeDtypeStruct(wg.shape, F32)
    d = jax.ShapeDtypeStruct(wd.shape, F32)
    half = jax.ShapeDtypeStruct((64, TILES * TOK, LANES), BF16)
    n = BLOCKS * 4
    rows = pltpu.VMEM((2, BLOCKS * CAP, 1024), BF16)
    return pl.pallas_call(
        gather_kernel,
        out_shape=(jax.ShapeDtypeStruct((128, MROWS, LANES), BF16), half, half, g, g, d),
        in_specs=[hbm, vmem, vmem, vmem],
        out_specs=(hbm, hbm, hbm, vmem, vmem, vmem),
        scratch_shapes=[pltpu.VMEM((2 * n, MROWS, LANES), BF16), rows, rows,
                        pltpu.VMEM((BLOCKS, 2 * CAP, 512), BF16), rows,
                        pltpu.VMEM((n, TILES * TOK, LANES), BF16),
                        dma, dma((3, 64, 2)), dma, dma((16,)), dma, dma((2, 2)), dma((2, 2)), dma],
        compiler_params=pltpu.CompilerParams(collective_id=0, has_side_effects=True, vmem_limit_bytes=60 * 1024 * 1024),
    )(msg, wg, wu, wd)


OFFSETS = ((2,), (1, -1), (0,))
EARLY = 4


def scatter_kernel(kept, given, out, mine, theirs, land, send_sem, recv_sem, load_sem, out_sem):
    me, core = where_am_i()
    greet(me, core)

    def prepare(r, pos):
        start, size = BACK[r]
        rows = pl.ds(start, size)
        mine[lin(pos), rows, :] = mine[lin(pos), rows, :] + theirs[lin(pos), rows, :]

    def slot(r, pos, phase):
        a = [pos[k] for k in ORDER[r]]
        return (20, 16 + a[0], a[0] * 4 + a[1])[phase]

    def hop(r, pos, phase, kind, d):
        half = None if kind else (0 if d == 1 else 1)
        start, size = rows_of(BACK, r, half)
        s = slot(r, pos, phase)
        lane = 2 if kind == 0 else (0 if d == 1 else 1)
        sem = (0 if d == 1 else 1) + 2 * kind
        return pltpu.make_async_remote_copy(
            src_ref=mine.at[lin(pos), pl.ds(start, size)],
            dst_ref=land.at[r, s * 3 + lane, pl.ds(start - BACK[r][0], size)],
            send_sem=send_sem, recv_sem=recv_sem.at[r, s, sem],
            device_id=dev_of(moved(me, ORDER[r][phase], d), core), device_id_type=MESH)

    def add(r, pos, phase, kind, d):
        hop(r, pos, phase, kind, d).wait_recv()
        half = None if kind else (0 if d == 1 else 1)
        start, size = rows_of(BACK, r, half)
        lane = 2 if kind == 0 else (0 if d == 1 else 1)
        rows = pl.ds(start, size)
        mine[lin(pos), rows, :] = (mine[lin(pos), rows, :]
                                   + land[r, slot(r, pos, phase) * 3 + lane, pl.ds(start - BACK[r][0], size), :])

    def far(r, base, phase):
        pos = moved(base, ORDER[r][phase], 2)
        if phase == 2:
            prepare(r, pos)
        for d in (1, -1):
            hop(r, pos, phase, 0, d).start()

    def near(r, base, phase):
        for d in (1, -1):
            pos = moved(base, ORDER[r][phase], d)
            if phase == 2:
                prepare(r, pos)
            add(r, pos, phase, 0, d)
            hop(r, pos, phase, 1, d).start()

    def here(r, base, phase):
        if phase == 2:
            prepare(r, base)
        for d in (1, -1):
            add(r, base, phase, 1, d)

    def order(i):
        return 2 + i

    def plane_base(r, i):
        return moved(moved(me, ORDER[r][0], order(i // 4)), ORDER[r][1], order(i % 4))

    def fetch(kind, i):
        for r in range(3):
            start, size = BACK[r]
            for o in OFFSETS[kind]:
                pos = moved(plane_base(r, i), ORDER[r][2], o)
                for src, dst in ((kept, mine), (given, theirs)):
                    pltpu.make_async_copy(src.at[lin(pos), pl.ds(start, size)], dst.at[lin(pos), pl.ds(start, size)],
                                          load_sem.at[kind, i]).start()

    def first(i, c):
        fetch(0, i)
        return c
    lax.fori_loop(0, EARLY, first, 0)
    for kind, step in enumerate((far, near, here)):
        def plane(i, c, kind=kind, step=step):
            n = 2 * len(OFFSETS[kind])
            pltpu.make_async_copy(mine.at[pl.ds(0, n)], mine.at[pl.ds(0, n)], load_sem.at[kind, i]).wait()
            for r in range(3):
                step(r, plane_base(r, i), 2)

            @pl.when(i + EARLY < 16)
            def _():
                fetch(kind, i + EARLY)
            if kind < 2:
                @pl.when(i + EARLY >= 16)
                def _():
                    fetch(kind + 1, i + EARLY - 16)
            return c
        lax.fori_loop(0, 16, plane, 0)
    for step in (far, near, here):
        def line(i, c, step=step):
            for r in range(3):
                step(r, moved(me, ORDER[r][0], order(i)), 1)
            return c
        lax.fori_loop(0, 4, line, 0)
    for step in (far, near, here):
        for r in range(3):
            step(r, me, 0)
    done = pltpu.make_async_copy(mine.at[lin(me)], out, out_sem)
    done.start()
    done.wait()
    most = theirs.at[pl.ds(0, 63)]
    pltpu.make_async_copy(most, most, send_sem).wait()


def scatter_all(kept, given):
    dma = pltpu.SemaphoreType.DMA
    rows = TILES * TOK
    return pl.pallas_call(
        scatter_kernel,
        out_shape=jax.ShapeDtypeStruct((rows, LANES), BF16),
        in_specs=[pl.BlockSpec(memory_space=pl.ANY)] * 2,
        out_specs=pl.BlockSpec(memory_space=pl.ANY),
        scratch_shapes=[pltpu.VMEM((64, rows, LANES), BF16), pltpu.VMEM((64, rows, LANES), BF16),
                        pltpu.VMEM((3, 63, 352, LANES), BF16),
                        dma, dma((3, 21, 4)), dma((3, 16)), dma],
        compiler_params=pltpu.CompilerParams(collective_id=1, has_side_effects=True, vmem_limit_bytes=60 * 1024 * 1024),
    )(kept, given)


def shards(tokens, out_grad, routes, gates, w_gate, w_up, w_down):
    y = lax.axis_index("mp")
    ids = jnp.arange(64, dtype=jnp.int32)
    named = jnp.sum((routes[:, :, None] == ids).astype(F32), axis=1)
    below = jnp.tril(jnp.ones((512, 512), F32), -1)
    before = jnp.dot(below.astype(BF16), named.astype(BF16), preferred_element_type=F32)
    before = jnp.sum(jnp.where(routes[:, :, None] == ids, before[:, None, :], 0.0), axis=2)
    own = lambda a: lax.dynamic_slice_in_dim(a, y * TOK, TOK, axis=0).T
    gate = own(gates)
    high = lax.reduce_precision(gate, 8, 7)
    meta = jnp.concatenate([own(routes).astype(F32), own(before), high, gate - high], axis=0).astype(BF16)
    tiled = lambda a: a.reshape(TOK, TILES, LANES).transpose(1, 0, 2)
    msg = jnp.concatenate([tiled(tokens), tiled(out_grad)], axis=1).reshape(META, LANES)
    msg = jnp.concatenate([msg, meta], axis=0)
    _, kept, given, grad_gate, grad_up, grad_down = gather_and_compute(msg, w_gate, w_up, w_down)
    back = scatter_all(kept, given)
    grad_tokens = back.reshape(TILES, TOK, LANES).transpose(1, 0, 2).reshape(TOK, TILES * LANES)
    return grad_tokens, grad_gate, grad_up, grad_down


def solution(mesh):
    in_specs = (
        P(("expert", "mp"), None),
        P(("expert", "mp"), None),
        P("expert", None),
        P("expert", None),
        P("expert", None, "mp"),
        P("expert", None, "mp"),
        P("expert", "mp", None),
    )
    out_specs = (
        P(("expert", "mp"), None),
        P("expert", None, "mp"),
        P("expert", None, "mp"),
        P("expert", "mp", None),
    )
    return jax.shard_map(shards, mesh=mesh, in_specs=in_specs, out_specs=out_specs, check_vma=False)
```

```python
import functools

import jax
import jax.numpy as jnp
from jax import lax
from jax.experimental import pallas as pl
from jax.experimental.pallas import tpu as pltpu
from jax.sharding import PartitionSpec as P

MESH = pl.DeviceIdType.MESH
BF16, F32 = jnp.bfloat16, jnp.float32
TOK, TILES, LANES = 128, 8, 128
CAP = 80
META = TILES * 2 * TOK
MROWS = META + 32
SPLIT = ((0, 688), (688, 688), (1376, 704))
BACK = ((0, 336), (336, 336), (672, 352))
ORDER = ((0, 1, 2), (1, 2, 0), (2, 0, 1))


def where_am_i():
    e = lax.axis_index("expert")
    return (e // 8, (e // 2) % 4, lax.axis_index("mp")), e % 2


def dev_of(pos, core):
    return ((pos[0] * 4 + pos[1]) * 2 + core, pos[2])


def index_of(pos, core):
    return ((pos[0] * 4 + pos[1]) * 2 + core) * 4 + pos[2]


def lin(pos):
    return (pos[0] * 4 + pos[1]) * 4 + pos[2]


def moved(pos, axis, by):
    p = list(pos)
    p[axis] = (p[axis] + by + 4) % 4
    return tuple(p)


def rows_of(split, r, half):
    start, size = split[r]
    low = (size // 32) * 16
    if half is None:
        return start, size
    return (start, low) if half == 0 else (start + low, size - low)


def greet(me, core):
    barrier = pltpu.get_barrier_semaphore()
    for axis in range(3):
        for d in (1, -1):
            pl.semaphore_signal(barrier, inc=1, device_id=dev_of(moved(me, axis, d), core), device_id_type=MESH)
    pl.semaphore_signal(barrier, inc=1, device_id=dev_of(me, 1 - core), device_id_type=MESH)
    pl.semaphore_wait(barrier, 7)


def tn(a, b):
    return lax.dot_general(a, b, (((0,), (0,)), ((), ())), preferred_element_type=F32)


def nt(a, b):
    return lax.dot_general(a, b, (((1,), (1,)), ((), ())), preferred_element_type=F32)


BLOCKS = 4
NEAR4 = (0, 1, 3, 2)
COL_Z = (0, 1, 3, 0, 0, 1, 3, 1, 3, 2, 0, 2, 1, 2, 3, 2)
COL_X = (0, 0, 0, 1, 3, 1, 1, 3, 3, 0, 2, 1, 2, 3, 2, 2)
AHEAD = 2
LOOK = 4


def entry(table, i):
    out = 0
    for k, v in enumerate(table):
        if v:
            out = out + jnp.where(i == k, v, 0)
    return out


def gather_kernel(msg, wg, wu, wd, buf, kept, gx, gd, slab, rows, away, ps, part, back, acts, stage, wx, wxt, wdt,
                  send_sem, recv_sem, own_sem, load_sem, rows_send, rows_recv, part_send, part_recv, stage_sem):
    me, core = where_am_i()
    other = dev_of(me, 1 - core)
    expert = lax.axis_index("expert")
    firsts = (2 * expert, 2 * (expert + 1 - 2 * core))
    greet(me, core)
    own = pltpu.make_async_copy(msg, buf.at[index_of(me, core)], own_sem)
    own.start()

    def ring(r, pos, half, axis, d, mine=False):
        start, size = rows_of(SPLIT, r, half)
        idx = index_of(pos, core)
        src = msg if mine else buf.at[idx]
        return pltpu.make_async_remote_copy(
            src_ref=src.at[pl.ds(start, size)], dst_ref=buf.at[idx, pl.ds(start, size)],
            send_sem=send_sem, recv_sem=recv_sem.at[r, lin(pos), 0 if half is None else half],
            device_id=dev_of(moved(me, axis, d), core), device_id_type=MESH)

    def send_full(r, pos, phases, mine=False):
        for p in phases:
            for d in (1, -1):
                ring(r, pos, None, ORDER[r][p], d, mine).start()

    def forward(r, base, phase):
        axis = ORDER[r][phase]
        for d in (1, -1):
            ring(r, moved(base, axis, -d), 0 if d == 1 else 1, axis, d).start()

    def near(r, base, phase, later=(), onward=True):
        axis = ORDER[r][phase]
        for d in (1, -1):
            pos = moved(base, axis, -d)
            ring(r, pos, None, axis, d).wait_recv()
            if onward:
                ring(r, pos, 0 if d == 1 else 1, axis, d).start()
            send_full(r, pos, later)

    def far(r, base, phase, later=()):
        axis = ORDER[r][phase]
        pos = moved(base, axis, 2)
        for half in (0, 1):
            ring(r, pos, half, axis, 1).wait_recv()
        send_full(r, pos, later)

    def column(i):
        return moved(moved(me, 0, entry(COL_Z, i)), 1, entry(COL_X, i))

    def base_of(r, i):
        return moved(moved(me, 1 if r == 1 else 0, entry(NEAR4, i // 4)), 2, entry(NEAR4, i % 4))

    def issue(u):
        def whole():
            for r in (1, 2):
                send_full(r, base_of(r, u), (2,))

        def halves():
            for r in (1, 2):
                for k in range(2):
                    forward(r, base_of(r, 2 * (u - 16) + k), 2)
        if isinstance(u, int):
            whole()
        else:
            pl.when(u < 16)(whole)
            pl.when((u >= 16) & (u < 24))(halves)

    for r in range(3):
        send_full(r, me, (0, 1, 2), mine=True)
    gx[...] = jnp.zeros_like(gx)
    gd[...] = jnp.zeros_like(gd)
    wx[:, :, 0:256] = wg[...]
    wx[:, :, 256:512] = wu[...]
    for j in range(2):
        wxt[j, 0:256] = wg[j].T
        wxt[j, 256:512] = wu[j].T
        wdt[j] = wd[j].T
    for r in range(3):
        near(r, me, 0, (1,))
    for r in range(3):
        far(r, me, 0, (1,))
    for i in (1,):
        send_full(0, column(i), (2,))

    def line(step):
        def body(i, c):
            for r in range(3):
                step(r, moved(me, ORDER[r][0], entry(NEAR4, i)), 1)
            return c
        return body
    lax.fori_loop(0, 4, line(near), 0)
    for u in (1, 2):
        issue(u)
    lax.fori_loop(0, 4, line(far), 0)

    own.wait()

    for u in range(3, LOOK):
        issue(u)
    def along_y(i):
        near(0, column(i), 2)

        @pl.when(i + AHEAD < 16)
        def _():
            send_full(0, column(i + AHEAD), (2,))

    def unit(u):
        @pl.when(u < 16)
        def _():
            for r in (1, 2):
                near(r, base_of(r, u), 2, onward=False)

        @pl.when((u >= 16) & (u < 24))
        def _():
            for r in (1, 2):
                for k in range(2):
                    far(r, base_of(r, 2 * (u - 16) + k), 2)
        issue(u + LOOK)

    def start_up(i, c):
        unit(i)
        pl.when(i < AHEAD - 1)(functools.partial(along_y, i))
        return c
    lax.fori_loop(0, 3, start_up, 0)

    slots = lax.broadcasted_iota(jnp.int32, (CAP, TOK), 0).astype(F32)

    def staged(k, at):
        return pltpu.make_async_copy(stage.at[pl.ds(k * 4, 4)], kept.at[pl.ds(pl.multiple_of(at * 4, 4), 4)], stage_sem.at[k])

    def send_rows(p, k):
        return pltpu.make_async_remote_copy(
            src_ref=away.at[k], dst_ref=rows.at[p % 2, 2 * k + core], send_sem=rows_send.at[k], recv_sem=rows_recv.at[k],
            device_id=other, device_id_type=MESH)

    def send_part(k):
        return pltpu.make_async_remote_copy(
            src_ref=part.at[2 * k + 1 - core], dst_ref=back.at[k], send_sem=part_send.at[k], recv_sem=part_recv.at[k],
            device_id=other, device_id_type=MESH)

    def pick(p, k):
        half = p % 2
        at = half * 8 + k * 4
        hots, gates = [[] for _ in range(4)], [0.0] * 4
        for y in range(4):
            meta = slab[at + y, pl.ds(META, 32), :].astype(F32)
            for j in range(4):
                named = (meta[0:8] == (firsts[j // 2] + j % 2).astype(F32)).astype(F32)
                where = jnp.sum(named * (meta[8:16] + 1.0), axis=0, keepdims=True) - 1.0
                gate = jnp.sum(named * (meta[16:24] + meta[24:32]), axis=0, keepdims=True)
                hot = (slots == where).astype(F32)
                hots[j].append(hot)
                gates[j] = gates[j] + hot * gate
        hot = jnp.concatenate([jnp.concatenate(h, axis=1) for h in hots], axis=0)
        gate = jnp.sum(jnp.concatenate(gates, axis=0), axis=1, keepdims=True)
        ps[k] = hot.T.astype(BF16)
        hot = hot.astype(BF16)
        for t in range(0, TILES, 2):
            for a in range(2):
                cols = jnp.concatenate([
                    jnp.concatenate([slab[at + y, pl.ds((t + u) * 2 * TOK + a * TOK, TOK), :] for u in range(2)], axis=1)
                    for y in range(4)], axis=0)
                got = jnp.dot(hot, cols, preferred_element_type=F32)
                got = (gate * got if a else got).astype(BF16)
                for j in range(2):
                    rows[half, 2 * k + core, a, j, :, pl.ds(t * LANES, 2 * LANES)] = got[j * CAP:(j + 1) * CAP]
                    away[k, a, j, :, pl.ds(t * LANES, 2 * LANES)] = got[(2 + j) * CAP:(3 + j) * CAP]

    def main(p, j):
        half = p % 2
        x = rows[half, :, 0, j].reshape(BLOCKS * CAP, 1024)
        s = rows[half, :, 1, j].reshape(BLOCKS * CAP, 1024)
        pre = jnp.dot(x, wx[j], preferred_element_type=F32)
        pre_gate, pre_up = pre[:, 0:256], pre[:, 256:512]
        d_hidden = jnp.dot(s, wdt[j], preferred_element_type=F32)
        sig = jax.nn.sigmoid(pre_gate)
        act = pre_gate * sig
        hidden = (act * pre_up).astype(BF16)
        d_up = (d_hidden * act).astype(BF16)
        d_gate = (d_hidden * pre_up * sig * (1.0 + pre_gate * (1.0 - sig))).astype(BF16)
        acts[j, :, 0:256] = hidden
        both = jnp.concatenate([d_gate, d_up], axis=1)
        acts[j, :, 256:768] = both
        part[:, j] = jnp.dot(both, wxt[j], preferred_element_type=F32).astype(BF16).reshape(BLOCKS, CAP, 1024)

    def weights(p, j):
        half = p % 2
        x = rows[half, :, 0, j].reshape(BLOCKS * CAP, 1024)
        s = rows[half, :, 1, j].reshape(BLOCKS * CAP, 1024)
        gd[j] += tn(acts[j, :, 0:256], s)
        gx[j] += tn(x, acts[j, :, 256:768])

    def place(k):
        hot = ps[k]
        for t in range(0, TILES, 2):
            cols = pl.ds(t * LANES, 2 * LANES)
            every = jnp.concatenate([part[2 * k + core, j, :, cols] for j in range(2)]
                                    + [back[k, j, :, cols] for j in range(2)], axis=0)
            out = jnp.dot(hot, every, preferred_element_type=F32).astype(BF16)
            for y in range(4):
                for u in range(2):
                    stage[k * 4 + y, pl.ds((t + u) * TOK, TOK), :] = out[y * TOK:(y + 1) * TOK, u * LANES:(u + 1) * LANES]

    def column_at(i):
        pos = column(i)
        return pos[0] * 4 + pos[1]

    def load(p, k):
        at = pl.multiple_of(column_at(2 * p + k) * 8 + core * 4, 4)
        half = p % 2
        return pltpu.make_async_copy(buf.at[pl.ds(at, 4)], slab.at[pl.ds(pl.multiple_of(half * 8 + k * 4, 4), 4)],
                                     load_sem.at[half, k])

    def compute(p, c):
        live, ready = p < 8, (p >= 1) & (p < 9)
        u = jnp.where(p < 5, 3 * p + 3, 2 * p + 8)
        unit(u)

        def picked(k):
            load(p - 1, k).wait()

            @pl.when(p >= 2)
            def _():
                send_rows(p, k).wait_send()
            pick(p - 1, k)
            send_rows(p - 1, k).start()
        pl.when(ready)(functools.partial(picked, 0))

        @pl.when(2 * p + AHEAD - 1 < 16)
        def _():
            along_y(2 * p + AHEAD - 1)
        unit(u + 1)
        pl.when(ready)(functools.partial(picked, 1))

        @pl.when(p >= 2)
        def _():
            for j in range(2):
                weights(p - 2, j)

        @pl.when(2 * p + AHEAD < 16)
        def _():
            along_y(2 * p + AHEAD)

        @pl.when(ready)
        def _():
            for k in range(2):
                send_rows(p - 1, k).wait_recv()

            @pl.when(p >= 2)
            def _():
                for k in range(2):
                    send_part(k).wait_send()
            for j in range(2):
                main(p - 1, j)
            for k in range(2):
                send_part(k).start()
        pl.when(p < 5)(lambda: unit(u + 2))

        @pl.when(live)
        def _():
            for k in range(2):
                far(0, column(2 * p + k), 2)
                load(p, k).start()

        @pl.when(ready)
        def _():
            @pl.when(p >= 2)
            def _():
                for k in range(2):
                    staged(k, 0).wait()
            for k in range(2):
                send_part(k).wait_recv()
                place(k)
                staged(k, column_at(2 * (p - 1) + k)).start()
        return c

    lax.fori_loop(0, 10, compute, 0)
    for k in range(2):
        staged(k, 0).wait()
        send_rows(0, k).wait_send()
        send_part(k).wait_send()
    most = buf.at[pl.ds(0, 63)]
    pltpu.make_async_copy(most, most, send_sem).wait()


def gather_and_compute(msg, wg, wu, wd):
    dma = pltpu.SemaphoreType.DMA
    hbm, vmem = pl.BlockSpec(memory_space=pl.ANY), pl.BlockSpec(memory_space=pltpu.VMEM)
    g = jax.ShapeDtypeStruct((2, 1024, 512), F32)
    d = jax.ShapeDtypeStruct(wd.shape, F32)
    bf = lambda *shape: pltpu.VMEM(shape, BF16)
    return pl.pallas_call(
        gather_kernel,
        out_shape=(jax.ShapeDtypeStruct((128, MROWS, LANES), BF16),
                   jax.ShapeDtypeStruct((64, TILES * TOK, LANES), BF16), g, d),
        in_specs=[vmem, vmem, vmem, vmem],
        out_specs=(hbm, hbm, vmem, vmem),
        scratch_shapes=[bf(16, MROWS, LANES), bf(2, BLOCKS, 2, 2, CAP, 1024), bf(2, 2, 2, CAP, 1024), bf(2, 512, 4 * CAP),
                        bf(BLOCKS, 2, CAP, 1024), bf(2, 2, CAP, 1024), bf(2, BLOCKS * CAP, 768), bf(8, TILES * TOK, LANES), bf(2, 1024, 512), bf(2, 512, 1024), bf(2, 1024, 256),
                        dma, dma((3, 64, 2)), dma, dma((2, 2)), dma((2,)), dma((2,)), dma((2,)), dma((2,)), dma((2,))],
        compiler_params=pltpu.CompilerParams(collective_id=0, has_side_effects=True, vmem_limit_bytes=60 * 1024 * 1024),
    )(msg, wg, wu, wd)


OFFSETS = ((2,), (1, -1), (0,))
EARLY = 4
LAG = 2
FAR4 = (2, 1, 3, 0)


def scatter_kernel(kept, out, mine, land, send_sem, recv_sem, load_sem, out_sem):
    me, core = where_am_i()
    greet(me, core)

    def slot(r, pos, phase):
        a = [pos[k] for k in ORDER[r]]
        return (20, 16 + a[0], a[0] * 4 + a[1])[phase]

    def hop(r, pos, phase, kind, d):
        half = None if kind else (0 if d == 1 else 1)
        start, size = rows_of(BACK, r, half)
        s = slot(r, pos, phase)
        lane = 2 if kind == 0 else (0 if d == 1 else 1)
        sem = (0 if d == 1 else 1) + 2 * kind
        return pltpu.make_async_remote_copy(
            src_ref=mine.at[lin(pos), pl.ds(start, size)],
            dst_ref=land.at[r, s * 3 + lane, pl.ds(start - BACK[r][0], size)],
            send_sem=send_sem, recv_sem=recv_sem.at[r, s, sem],
            device_id=dev_of(moved(me, ORDER[r][phase], d), core), device_id_type=MESH)

    def add(r, pos, phase, kind, d):
        hop(r, pos, phase, kind, d).wait_recv()
        half = None if kind else (0 if d == 1 else 1)
        start, size = rows_of(BACK, r, half)
        lane = 2 if kind == 0 else (0 if d == 1 else 1)
        rows = pl.ds(start, size)
        mine[lin(pos), rows, :] = (mine[lin(pos), rows, :]
                                   + land[r, slot(r, pos, phase) * 3 + lane, pl.ds(start - BACK[r][0], size), :])

    def far(r, base, phase):
        pos = moved(base, ORDER[r][phase], 2)
        for d in (1, -1):
            hop(r, pos, phase, 0, d).start()

    def near(r, base, phase):
        for d in (1, -1):
            pos = moved(base, ORDER[r][phase], d)
            add(r, pos, phase, 0, d)
            hop(r, pos, phase, 1, d).start()

    def here(r, base, phase):
        for d in (1, -1):
            add(r, base, phase, 1, d)

    def plane_base(r, i):
        return moved(moved(me, ORDER[r][0], entry(FAR4, i // 4)), ORDER[r][1], entry(FAR4, i % 4))

    def lines(step, l):
        for r in range(3):
            step(r, moved(me, ORDER[r][0], entry(FAR4, l)), 1)

    def ends(step):
        for r in range(3):
            step(r, me, 0)

    def fetch(kind, i):
        for r in range(3):
            start, size = BACK[r]
            for o in OFFSETS[kind]:
                pos = moved(plane_base(r, i), ORDER[r][2], o)
                pltpu.make_async_copy(kept.at[lin(pos), pl.ds(start, size)], mine.at[lin(pos), pl.ds(start, size)],
                                      load_sem.at[kind, i]).start()

    for kind in range(3):
        for i in range(EARLY - kind * LAG):
            fetch(kind, i)

    def plane(i, c):
        for kind, step in enumerate((far, near, here)):
            k = i - kind * LAG

            @pl.when((k + EARLY < 16) & (k + EARLY >= 0))
            def _(kind=kind, k=k):
                fetch(kind, k + EARLY)
        for kind, step in enumerate((far, near, here)):
            k = i - kind * LAG

            @pl.when((k >= 0) & (k < 16))
            def _(kind=kind, k=k, step=step):
                n = len(OFFSETS[kind])
                pltpu.make_async_copy(mine.at[pl.ds(0, n)], mine.at[pl.ds(0, n)], load_sem.at[kind, k]).wait()
                for r in range(3):
                    step(r, plane_base(r, k), 2)
        k = i - 2 * LAG
        for l in range(4):
            @pl.when(k == 4 * l + 3)
            def _(l=l):
                lines(far, l)
                if l >= 1:
                    lines(near, l - 1)
                if l >= 2:
                    lines(here, l - 2)
                if l == 2:
                    ends(far)
        return c
    lax.fori_loop(0, 16 + 2 * LAG, plane, 0)
    lines(here, 2)
    ends(near)
    lines(near, 3)
    lines(here, 3)
    ends(here)
    done = pltpu.make_async_copy(mine.at[lin(me)], out, out_sem)
    done.start()
    done.wait()
    most = mine.at[pl.ds(0, 63)]
    pltpu.make_async_copy(most, most, send_sem).wait()


def scatter_all(kept):
    dma = pltpu.SemaphoreType.DMA
    rows = TILES * TOK
    return pl.pallas_call(
        scatter_kernel,
        out_shape=jax.ShapeDtypeStruct((rows, LANES), BF16),
        in_specs=[pl.BlockSpec(memory_space=pl.ANY)],
        out_specs=pl.BlockSpec(memory_space=pl.ANY),
        scratch_shapes=[pltpu.VMEM((64, rows, LANES), BF16),
                        pltpu.VMEM((3, 63, 352, LANES), BF16),
                        dma, dma((3, 21, 4)), dma((3, 16)), dma],
        compiler_params=pltpu.CompilerParams(collective_id=1, has_side_effects=True, vmem_limit_bytes=60 * 1024 * 1024),
    )(kept)


def shards(tokens, out_grad, routes, gates, w_gate, w_up, w_down):
    y = lax.axis_index("mp")
    ids = jnp.arange(64, dtype=jnp.int32)
    named = jnp.sum((routes[:, :, None] == ids).astype(F32), axis=1)
    below = jnp.tril(jnp.ones((512, 512), F32), -1)
    before = jnp.dot(below.astype(BF16), named.astype(BF16), preferred_element_type=F32)
    before = jnp.sum(jnp.where(routes[:, :, None] == ids, before[:, None, :], 0.0), axis=2)
    own = lambda a: lax.dynamic_slice_in_dim(a, y * TOK, TOK, axis=0).T
    gate = own(gates)
    high = lax.reduce_precision(gate, 8, 7)
    meta = jnp.concatenate([own(routes).astype(F32), own(before), high, gate - high], axis=0).astype(BF16)
    tiled = lambda a: a.reshape(TOK, TILES, LANES).transpose(1, 0, 2)
    msg = jnp.concatenate([tiled(tokens), tiled(out_grad)], axis=1).reshape(META, LANES)
    msg = jnp.concatenate([msg, meta], axis=0)
    _, kept, both, grad_down = gather_and_compute(msg, w_gate, w_up, w_down)
    grad_gate, grad_up = both[:, :, 0:256], both[:, :, 256:512]
    back = scatter_all(kept)
    grad_tokens = back.reshape(TILES, TOK, LANES).transpose(1, 0, 2).reshape(TOK, TILES * LANES)
    return grad_tokens, grad_gate, grad_up, grad_down


def solution(mesh):
    in_specs = (
        P(("expert", "mp"), None),
        P(("expert", "mp"), None),
        P("expert", None),
        P("expert", None),
        P("expert", None, "mp"),
        P("expert", None, "mp"),
        P("expert", "mp", None),
    )
    out_specs = (
        P(("expert", "mp"), None),
        P("expert", None, "mp"),
        P("expert", None, "mp"),
        P("expert", "mp", None),
    )
    return jax.shard_map(shards, mesh=mesh, in_specs=in_specs, out_specs=out_specs, check_vma=False)
```

```python
import functools

import jax
import jax.numpy as jnp
from jax import lax
from jax.experimental import pallas as pl
from jax.experimental.pallas import tpu as pltpu
from jax.sharding import PartitionSpec as P

MESH = pl.DeviceIdType.MESH
BF16, F32 = jnp.bfloat16, jnp.float32
TOK, TILES, LANES = 128, 8, 128
CAP = 80
META = TILES * 2 * TOK
MROWS = META + 32
SPLIT = ((0, 688), (688, 688), (1376, 704))
BACK = ((0, 336), (336, 336), (672, 352))
ORDER = ((0, 1, 2), (1, 2, 0), (2, 0, 1))


def where_am_i():
    e = lax.axis_index("expert")
    return (e // 8, (e // 2) % 4, lax.axis_index("mp")), e % 2


def dev_of(pos, core):
    return ((pos[0] * 4 + pos[1]) * 2 + core, pos[2])


def index_of(pos, core):
    return ((pos[0] * 4 + pos[1]) * 2 + core) * 4 + pos[2]


def lin(pos):
    return (pos[0] * 4 + pos[1]) * 4 + pos[2]


def moved(pos, axis, by):
    p = list(pos)
    p[axis] = (p[axis] + by + 4) % 4
    return tuple(p)


def rows_of(split, r, half):
    start, size = split[r]
    low = (size // 32) * 16
    if half is None:
        return start, size
    return (start, low) if half == 0 else (start + low, size - low)


def greet(me, core):
    barrier = pltpu.get_barrier_semaphore()
    for axis in range(3):
        for d in (1, -1):
            pl.semaphore_signal(barrier, inc=1, device_id=dev_of(moved(me, axis, d), core), device_id_type=MESH)
    pl.semaphore_signal(barrier, inc=1, device_id=dev_of(me, 1 - core), device_id_type=MESH)
    pl.semaphore_wait(barrier, 7)


def tn(a, b):
    return lax.dot_general(a, b, (((0,), (0,)), ((), ())), preferred_element_type=F32)


def nt(a, b):
    return lax.dot_general(a, b, (((1,), (1,)), ((), ())), preferred_element_type=F32)


BLOCKS = 4
NEAR4 = (0, 1, 3, 2)
COL_Z = (0, 1, 3, 0, 0, 1, 3, 1, 3, 2, 0, 2, 1, 2, 3, 2)
COL_X = (0, 0, 0, 1, 3, 1, 1, 3, 3, 0, 2, 1, 2, 3, 2, 2)
AHEAD = 2
LOOK = 4


def entry(table, i):
    out = 0
    for k, v in enumerate(table):
        if v:
            out = out + jnp.where(i == k, v, 0)
    return out


def gather_kernel(msg, wg, wu, wd, buf, kept, gx, gd, slab, rows, away, ps, part, back, acts, stage, wx, wxt, wdt,
                  send_sem, recv_sem, own_sem, load_sem, rows_send, rows_recv, part_send, part_recv, stage_sem):
    me, core = where_am_i()
    other = dev_of(me, 1 - core)
    expert = lax.axis_index("expert")
    firsts = (2 * expert, 2 * (expert + 1 - 2 * core))
    greet(me, core)
    own = pltpu.make_async_copy(msg, buf.at[index_of(me, core)], own_sem)
    own.start()

    def ring(r, pos, half, axis, d, mine=False):
        start, size = rows_of(SPLIT, r, half)
        idx = index_of(pos, core)
        src = msg if mine else buf.at[idx]
        return pltpu.make_async_remote_copy(
            src_ref=src.at[pl.ds(start, size)], dst_ref=buf.at[idx, pl.ds(start, size)],
            send_sem=send_sem, recv_sem=recv_sem.at[r, lin(pos), 0 if half is None else half],
            device_id=dev_of(moved(me, axis, d), core), device_id_type=MESH)

    def send_full(r, pos, phases, mine=False):
        for p in phases:
            for d in (1, -1):
                ring(r, pos, None, ORDER[r][p], d, mine).start()

    def forward(r, base, phase):
        axis = ORDER[r][phase]
        for d in (1, -1):
            ring(r, moved(base, axis, -d), 0 if d == 1 else 1, axis, d).start()

    def near(r, base, phase, later=(), onward=True):
        axis = ORDER[r][phase]
        for d in (1, -1):
            pos = moved(base, axis, -d)
            ring(r, pos, None, axis, d).wait_recv()
            if onward:
                ring(r, pos, 0 if d == 1 else 1, axis, d).start()
            send_full(r, pos, later)

    def far(r, base, phase, later=()):
        axis = ORDER[r][phase]
        pos = moved(base, axis, 2)
        for half in (0, 1):
            ring(r, pos, half, axis, 1).wait_recv()
        send_full(r, pos, later)

    def column(i):
        return moved(moved(me, 0, entry(COL_Z, i)), 1, entry(COL_X, i))

    def base_of(r, i):
        return moved(moved(me, 1 if r == 1 else 0, entry(NEAR4, i // 4)), 2, entry(NEAR4, i % 4))

    def issue(u):
        def whole():
            for r in (1, 2):
                send_full(r, base_of(r, u), (2,))

        def halves():
            for r in (1, 2):
                for k in range(2):
                    forward(r, base_of(r, 2 * (u - 16) + k), 2)
        if isinstance(u, int):
            whole()
        else:
            pl.when(u < 16)(whole)
            pl.when((u >= 16) & (u < 24))(halves)

    for r in range(3):
        send_full(r, me, (0, 1, 2), mine=True)
    gx[...] = jnp.zeros_like(gx)
    gd[...] = jnp.zeros_like(gd)
    wx[:, :, 0:256] = wg[...]
    wx[:, :, 256:512] = wu[...]
    for j in range(2):
        wxt[j, 0:256] = wg[j].T
        wxt[j, 256:512] = wu[j].T
        wdt[j] = wd[j].T
    for r in range(3):
        near(r, me, 0, (1,))
    for r in range(3):
        far(r, me, 0, (1,))
    for i in (1,):
        send_full(0, column(i), (2,))

    def line(step):
        def body(i, c):
            for r in range(3):
                step(r, moved(me, ORDER[r][0], entry(NEAR4, i)), 1)
            return c
        return body
    lax.fori_loop(0, 4, line(near), 0)
    for u in (1, 2):
        issue(u)
    lax.fori_loop(0, 4, line(far), 0)

    own.wait()

    for u in range(3, LOOK):
        issue(u)
    def along_y(i):
        near(0, column(i), 2)

        @pl.when(i + AHEAD < 16)
        def _():
            send_full(0, column(i + AHEAD), (2,))

    def unit(u):
        @pl.when(u < 16)
        def _():
            for r in (1, 2):
                near(r, base_of(r, u), 2, onward=False)

        @pl.when((u >= 16) & (u < 24))
        def _():
            for r in (1, 2):
                for k in range(2):
                    far(r, base_of(r, 2 * (u - 16) + k), 2)
        issue(u + LOOK)

    def start_up(i, c):
        unit(i)
        pl.when(i < AHEAD - 1)(functools.partial(along_y, i))
        return c
    lax.fori_loop(0, 3, start_up, 0)

    slots = lax.broadcasted_iota(jnp.int32, (CAP, TOK), 0).astype(F32)

    def staged(k, at):
        return pltpu.make_async_copy(stage.at[pl.ds(k * 4, 4)], kept.at[pl.ds(pl.multiple_of(at * 4, 4), 4)], stage_sem.at[k])

    def send_rows(p, k):
        return pltpu.make_async_remote_copy(
            src_ref=away.at[k], dst_ref=rows.at[p % 2, 2 * k + core], send_sem=rows_send.at[k], recv_sem=rows_recv.at[k],
            device_id=other, device_id_type=MESH)

    def send_part(k):
        return pltpu.make_async_remote_copy(
            src_ref=part.at[2 * k + 1 - core], dst_ref=back.at[k], send_sem=part_send.at[k], recv_sem=part_recv.at[k],
            device_id=other, device_id_type=MESH)

    def pick(p, k):
        half = p % 2
        at = half * 8 + k * 4
        hots, gates = [[] for _ in range(4)], [0.0] * 4
        for y in range(4):
            meta = slab[at + y, pl.ds(META, 32), :].astype(F32)
            for j in range(4):
                named = (meta[0:8] == (firsts[j // 2] + j % 2).astype(F32)).astype(F32)
                where = jnp.sum(named * (meta[8:16] + 1.0), axis=0, keepdims=True) - 1.0
                gate = jnp.sum(named * (meta[16:24] + meta[24:32]), axis=0, keepdims=True)
                hot = (slots == where).astype(F32)
                hots[j].append(hot)
                gates[j] = gates[j] + hot * gate
        hot = jnp.concatenate([jnp.concatenate(h, axis=1) for h in hots], axis=0)
        gate = jnp.sum(jnp.concatenate(gates, axis=0), axis=1, keepdims=True)
        ps[k] = hot.T.astype(BF16)
        hot = hot.astype(BF16)
        for t in range(0, TILES, 2):
            for a in range(2):
                cols = jnp.concatenate([
                    jnp.concatenate([slab[at + y, pl.ds((t + u) * 2 * TOK + a * TOK, TOK), :] for u in range(2)], axis=1)
                    for y in range(4)], axis=0)
                got = jnp.dot(hot, cols, preferred_element_type=F32)
                got = (gate * got if a else got).astype(BF16)
                for j in range(2):
                    rows[half, 2 * k + core, a, j, :, pl.ds(t * LANES, 2 * LANES)] = got[j * CAP:(j + 1) * CAP]
                    away[k, a, j, :, pl.ds(t * LANES, 2 * LANES)] = got[(2 + j) * CAP:(3 + j) * CAP]

    def main(p, j):
        half = p % 2
        x = rows[half, :, 0, j].reshape(BLOCKS * CAP, 1024)
        s = rows[half, :, 1, j].reshape(BLOCKS * CAP, 1024)
        pre = jnp.dot(x, wx[j], preferred_element_type=F32)
        pre_gate, pre_up = pre[:, 0:256], pre[:, 256:512]
        d_hidden = jnp.dot(s, wdt[j], preferred_element_type=F32)
        sig = jax.nn.sigmoid(pre_gate)
        act = pre_gate * sig
        hidden = (act * pre_up).astype(BF16)
        d_up = (d_hidden * act).astype(BF16)
        d_gate = (d_hidden * pre_up * sig * (1.0 + pre_gate * (1.0 - sig))).astype(BF16)
        acts[j, :, 0:256] = hidden
        both = jnp.concatenate([d_gate, d_up], axis=1)
        acts[j, :, 256:768] = both
        part[:, j] = jnp.dot(both, wxt[j], preferred_element_type=F32).astype(BF16).reshape(BLOCKS, CAP, 1024)

    def weights(p, j):
        half = p % 2
        x = rows[half, :, 0, j].reshape(BLOCKS * CAP, 1024)
        s = rows[half, :, 1, j].reshape(BLOCKS * CAP, 1024)
        gd[j] += tn(acts[j, :, 0:256], s)
        gx[j] += tn(x, acts[j, :, 256:768])

    def place(k):
        hot = ps[k]
        for t in range(0, TILES, 2):
            cols = pl.ds(t * LANES, 2 * LANES)
            every = jnp.concatenate([part[2 * k + core, j, :, cols] for j in range(2)]
                                    + [back[k, j, :, cols] for j in range(2)], axis=0)
            out = jnp.dot(hot, every, preferred_element_type=F32).astype(BF16)
            for y in range(4):
                for u in range(2):
                    stage[k * 4 + y, pl.ds((t + u) * TOK, TOK), :] = out[y * TOK:(y + 1) * TOK, u * LANES:(u + 1) * LANES]

    def column_at(i):
        pos = column(i)
        return pos[0] * 4 + pos[1]

    def load(p, k):
        at = pl.multiple_of(column_at(2 * p + k) * 8 + core * 4, 4)
        half = p % 2
        return pltpu.make_async_copy(buf.at[pl.ds(at, 4)], slab.at[pl.ds(pl.multiple_of(half * 8 + k * 4, 4), 4)],
                                     load_sem.at[half, k])

    def compute(p, c):
        live, ready = p < 8, (p >= 1) & (p < 9)
        u = jnp.where(p < 5, 3 * p + 3, 2 * p + 8)
        unit(u)

        def picked(k):
            load(p - 1, k).wait()

            @pl.when(p >= 2)
            def _():
                send_rows(p, k).wait_send()
            pick(p - 1, k)
            send_rows(p - 1, k).start()
        pl.when(ready)(functools.partial(picked, 0))

        @pl.when(2 * p + AHEAD - 1 < 16)
        def _():
            along_y(2 * p + AHEAD - 1)
        unit(u + 1)
        pl.when(ready)(functools.partial(picked, 1))

        @pl.when(p >= 2)
        def _():
            for j in range(2):
                weights(p - 2, j)

        @pl.when(2 * p + AHEAD < 16)
        def _():
            along_y(2 * p + AHEAD)

        @pl.when(ready)
        def _():
            for k in range(2):
                send_rows(p - 1, k).wait_recv()

            @pl.when(p >= 2)
            def _():
                for k in range(2):
                    send_part(k).wait_send()
            for j in range(2):
                main(p - 1, j)
            for k in range(2):
                send_part(k).start()
        pl.when(p < 5)(lambda: unit(u + 2))

        @pl.when(live)
        def _():
            for k in range(2):
                far(0, column(2 * p + k), 2)
                load(p, k).start()

        @pl.when(ready)
        def _():
            @pl.when(p >= 2)
            def _():
                for k in range(2):
                    staged(k, 0).wait()
            for k in range(2):
                send_part(k).wait_recv()
                place(k)
                staged(k, column_at(2 * (p - 1) + k)).start()
        return c

    lax.fori_loop(0, 10, compute, 0)
    for k in range(2):
        staged(k, 0).wait()
        send_rows(0, k).wait_send()
        send_part(k).wait_send()
    most = buf.at[pl.ds(0, 63)]
    pltpu.make_async_copy(most, most, send_sem).wait()


def gather_and_compute(msg, wg, wu, wd):
    dma = pltpu.SemaphoreType.DMA
    hbm, vmem = pl.BlockSpec(memory_space=pl.ANY), pl.BlockSpec(memory_space=pltpu.VMEM)
    g = jax.ShapeDtypeStruct((2, 1024, 512), F32)
    d = jax.ShapeDtypeStruct(wd.shape, F32)
    bf = lambda *shape: pltpu.VMEM(shape, BF16)
    return pl.pallas_call(
        gather_kernel,
        out_shape=(jax.ShapeDtypeStruct((128, MROWS, LANES), BF16),
                   jax.ShapeDtypeStruct((64, TILES * TOK, LANES), BF16), g, d),
        in_specs=[vmem, vmem, vmem, vmem],
        out_specs=(hbm, hbm, vmem, vmem),
        scratch_shapes=[bf(16, MROWS, LANES), bf(2, BLOCKS, 2, 2, CAP, 1024), bf(2, 2, 2, CAP, 1024), bf(2, 512, 4 * CAP),
                        bf(BLOCKS, 2, CAP, 1024), bf(2, 2, CAP, 1024), bf(2, BLOCKS * CAP, 768), bf(8, TILES * TOK, LANES), bf(2, 1024, 512), bf(2, 512, 1024), bf(2, 1024, 256),
                        dma, dma((3, 64, 2)), dma, dma((2, 2)), dma((2,)), dma((2,)), dma((2,)), dma((2,)), dma((2,))],
        compiler_params=pltpu.CompilerParams(collective_id=0, has_side_effects=True, vmem_limit_bytes=60 * 1024 * 1024),
    )(msg, wg, wu, wd)


OFFSETS = ((2,), (1, -1), (0,))
EARLY = 4
LAG = 2
FAR4 = (2, 1, 3, 0)


def scatter_kernel(kept, out, mine, land, send_sem, recv_sem, load_sem, out_sem):
    me, core = where_am_i()
    greet(me, core)

    def slot(r, pos, phase):
        a = [pos[k] for k in ORDER[r]]
        return (20, 16 + a[0], a[0] * 4 + a[1])[phase]

    def hop(r, pos, phase, kind, d):
        half = None if kind else (0 if d == 1 else 1)
        start, size = rows_of(BACK, r, half)
        s = slot(r, pos, phase)
        lane = 2 if kind == 0 else (0 if d == 1 else 1)
        sem = (0 if d == 1 else 1) + 2 * kind
        return pltpu.make_async_remote_copy(
            src_ref=mine.at[lin(pos), pl.ds(start, size)],
            dst_ref=land.at[r, s * 3 + lane, pl.ds(start - BACK[r][0], size)],
            send_sem=send_sem, recv_sem=recv_sem.at[r, s, sem],
            device_id=dev_of(moved(me, ORDER[r][phase], d), core), device_id_type=MESH)

    def add(r, pos, phase, kind, d):
        hop(r, pos, phase, kind, d).wait_recv()
        half = None if kind else (0 if d == 1 else 1)
        start, size = rows_of(BACK, r, half)
        lane = 2 if kind == 0 else (0 if d == 1 else 1)
        rows = pl.ds(start, size)
        mine[lin(pos), rows, :] = (mine[lin(pos), rows, :]
                                   + land[r, slot(r, pos, phase) * 3 + lane, pl.ds(start - BACK[r][0], size), :])

    def far(r, base, phase):
        pos = moved(base, ORDER[r][phase], 2)
        for d in (1, -1):
            hop(r, pos, phase, 0, d).start()

    def near(r, base, phase):
        for d in (1, -1):
            pos = moved(base, ORDER[r][phase], d)
            add(r, pos, phase, 0, d)
            hop(r, pos, phase, 1, d).start()

    def here(r, base, phase):
        for d in (1, -1):
            add(r, base, phase, 1, d)

    def plane_base(r, i):
        return moved(moved(me, ORDER[r][0], entry(FAR4, i // 4)), ORDER[r][1], entry(FAR4, i % 4))

    def lines(step, l):
        for r in range(3):
            step(r, moved(me, ORDER[r][0], entry(FAR4, l)), 1)

    def ends(step):
        for r in range(3):
            step(r, me, 0)

    def fetch(kind, i):
        for r in range(3):
            start, size = BACK[r]
            for o in OFFSETS[kind]:
                pos = moved(plane_base(r, i), ORDER[r][2], o)
                pltpu.make_async_copy(kept.at[lin(pos), pl.ds(start, size)], mine.at[lin(pos), pl.ds(start, size)],
                                      load_sem.at[kind, i]).start()

    for kind in range(3):
        for i in range(EARLY - kind * LAG):
            fetch(kind, i)

    def plane(i, c):
        for kind, step in enumerate((far, near, here)):
            k = i - kind * LAG

            @pl.when((k + EARLY < 16) & (k + EARLY >= 0))
            def _(kind=kind, k=k):
                fetch(kind, k + EARLY)
        for kind, step in enumerate((far, near, here)):
            k = i - kind * LAG

            @pl.when((k >= 0) & (k < 16))
            def _(kind=kind, k=k, step=step):
                n = len(OFFSETS[kind])
                pltpu.make_async_copy(mine.at[pl.ds(0, n)], mine.at[pl.ds(0, n)], load_sem.at[kind, k]).wait()
                for r in range(3):
                    step(r, plane_base(r, k), 2)
        k = i - 2 * LAG
        for l in range(4):
            @pl.when(k == 4 * l + 3)
            def _(l=l):
                lines(far, l)
                if l >= 1:
                    lines(near, l - 1)
                if l >= 2:
                    lines(here, l - 2)
                if l == 2:
                    ends(far)
        return c
    lax.fori_loop(0, 16 + 2 * LAG, plane, 0)
    lines(here, 2)
    ends(near)
    lines(near, 3)
    lines(here, 3)
    ends(here)
    done = pltpu.make_async_copy(mine.at[lin(me)], out, out_sem)
    done.start()
    done.wait()
    most = mine.at[pl.ds(0, 63)]
    pltpu.make_async_copy(most, most, send_sem).wait()


def scatter_all(kept):
    dma = pltpu.SemaphoreType.DMA
    rows = TILES * TOK
    return pl.pallas_call(
        scatter_kernel,
        out_shape=jax.ShapeDtypeStruct((rows, LANES), BF16),
        in_specs=[pl.BlockSpec(memory_space=pl.ANY)],
        out_specs=pl.BlockSpec(memory_space=pl.ANY),
        scratch_shapes=[pltpu.VMEM((64, rows, LANES), BF16),
                        pltpu.VMEM((3, 63, 352, LANES), BF16),
                        dma, dma((3, 21, 4)), dma((3, 16)), dma],
        compiler_params=pltpu.CompilerParams(collective_id=1, has_side_effects=True, vmem_limit_bytes=60 * 1024 * 1024),
    )(kept)


PIECES = 2


def write_kernel(both, down, back, tokens_out, gate_out, up_out, down_out):
    @pl.when(pl.program_id(0) == 0)
    def _():
        for t in range(TILES):
            tokens_out[:, t * LANES:(t + 1) * LANES] = back[t * TOK:(t + 1) * TOK, :]
    gate_out[...] = both[:, :, 0:256]
    up_out[...] = both[:, :, 256:512]
    down_out[...] = down[...]


def write_all(both, down, back):
    piece = lambda r, c: pl.BlockSpec((1, r // PIECES, c), lambda i: (i // PIECES, i % PIECES, 0))
    whole = lambda *shape: pl.BlockSpec(shape, lambda i: (0, 0))
    return pl.pallas_call(
        write_kernel,
        grid=(2 * PIECES,),
        out_shape=(jax.ShapeDtypeStruct((TOK, TILES * LANES), BF16), jax.ShapeDtypeStruct((2, 1024, 256), F32),
                   jax.ShapeDtypeStruct((2, 1024, 256), F32), jax.ShapeDtypeStruct((2, 256, 1024), F32)),
        in_specs=[piece(1024, 512), piece(256, 1024), whole(TILES * TOK, LANES)],
        out_specs=(whole(TOK, TILES * LANES), piece(1024, 256), piece(1024, 256), piece(256, 1024)),
        compiler_params=pltpu.CompilerParams(vmem_limit_bytes=32 * 1024 * 1024),
    )(both, down, back)


def shards(tokens, out_grad, routes, gates, w_gate, w_up, w_down):
    y = lax.axis_index("mp")
    ids = jnp.arange(64, dtype=jnp.int32)
    named = jnp.sum((routes[:, :, None] == ids).astype(F32), axis=1)
    below = jnp.tril(jnp.ones((512, 512), F32), -1)
    before = jnp.dot(below.astype(BF16), named.astype(BF16), preferred_element_type=F32)
    before = jnp.sum(jnp.where(routes[:, :, None] == ids, before[:, None, :], 0.0), axis=2)
    own = lambda a: lax.dynamic_slice_in_dim(a, y * TOK, TOK, axis=0).T
    gate = own(gates)
    high = lax.reduce_precision(gate, 8, 7)
    meta = jnp.concatenate([own(routes).astype(F32), own(before), high, gate - high], axis=0).astype(BF16)
    tiled = lambda a: a.reshape(TOK, TILES, LANES).transpose(1, 0, 2)
    msg = jnp.concatenate([tiled(tokens), tiled(out_grad)], axis=1).reshape(META, LANES)
    msg = jnp.concatenate([msg, meta], axis=0)
    _, kept, both, grad_down = gather_and_compute(msg, w_gate, w_up, w_down)
    return write_all(both, grad_down, scatter_all(kept))


def solution(mesh):
    in_specs = (
        P(("expert", "mp"), None),
        P(("expert", "mp"), None),
        P("expert", None),
        P("expert", None),
        P("expert", None, "mp"),
        P("expert", None, "mp"),
        P("expert", "mp", None),
    )
    out_specs = (
        P(("expert", "mp"), None),
        P("expert", None, "mp"),
        P("expert", None, "mp"),
        P("expert", "mp", None),
    )
    return jax.shard_map(shards, mesh=mesh, in_specs=in_specs, out_specs=out_specs, check_vma=False)
```

```python
import functools

import jax
import jax.numpy as jnp
from jax import lax
from jax.experimental import pallas as pl
from jax.experimental.pallas import tpu as pltpu
from jax.sharding import PartitionSpec as P

MESH = pl.DeviceIdType.MESH
BF16, F32 = jnp.bfloat16, jnp.float32
TOK, TILES, LANES = 128, 8, 128
CAP = 80
META = TILES * 2 * TOK
MROWS = META + 32
SPLIT = ((0, 688), (688, 688), (1376, 704))
BACK = ((0, 336), (336, 336), (672, 352))
ORDER = ((0, 1, 2), (1, 2, 0), (2, 0, 1))


def where_am_i():
    e = lax.axis_index("expert")
    return (e // 8, (e // 2) % 4, lax.axis_index("mp")), e % 2


def dev_of(pos, core):
    return ((pos[0] * 4 + pos[1]) * 2 + core, pos[2])


def index_of(pos, core):
    return ((pos[0] * 4 + pos[1]) * 2 + core) * 4 + pos[2]


def lin(pos):
    return (pos[0] * 4 + pos[1]) * 4 + pos[2]


def moved(pos, axis, by):
    p = list(pos)
    p[axis] = (p[axis] + by + 4) % 4
    return tuple(p)


def rows_of(split, r, half):
    start, size = split[r]
    low = (size // 32) * 16
    if half is None:
        return start, size
    return (start, low) if half == 0 else (start + low, size - low)


def greet(me, core):
    barrier = pltpu.get_barrier_semaphore()
    for axis in range(3):
        for d in (1, -1):
            pl.semaphore_signal(barrier, inc=1, device_id=dev_of(moved(me, axis, d), core), device_id_type=MESH)
    pl.semaphore_signal(barrier, inc=1, device_id=dev_of(me, 1 - core), device_id_type=MESH)
    pl.semaphore_wait(barrier, 7)


def tn(a, b):
    return lax.dot_general(a, b, (((0,), (0,)), ((), ())), preferred_element_type=F32)


def nt(a, b):
    return lax.dot_general(a, b, (((1,), (1,)), ((), ())), preferred_element_type=F32)


BLOCKS = 4
NEAR4 = (0, 1, 3, 2)
COL_Z = (0, 1, 3, 0, 0, 1, 3, 1, 3, 2, 0, 2, 1, 2, 3, 2)
COL_X = (0, 0, 0, 1, 3, 1, 1, 3, 3, 0, 2, 1, 2, 3, 2, 2)
AHEAD = 2
LOOK = 4


def entry(table, i):
    out = 0
    for k, v in enumerate(table):
        if v:
            out = out + jnp.where(i == k, v, 0)
    return out


def gather_kernel(x_in, dy_in, meta_in, wg_in, wu_in, wd_in, buf, kept, gx, gd, slab, rows, away, ps, part, back, acts, stage, wx, wxt, wdt, msg, wg, wu, wd, w_sem,
                  send_sem, recv_sem, own_sem, load_sem, rows_send, rows_recv, part_send, part_recv, stage_sem):
    me, core = where_am_i()
    other = dev_of(me, 1 - core)
    expert = lax.axis_index("expert")
    firsts = (2 * expert, 2 * (expert + 1 - 2 * core))
    weights_in = [pltpu.make_async_copy(src, dst, w_sem.at[i])
                  for i, (src, dst) in enumerate(((wg_in, wg), (wu_in, wu), (wd_in, wd)))]
    for copy in weights_in:
        copy.start()
    for t in range(TILES):
        cols = slice(t * LANES, (t + 1) * LANES)
        msg[2 * t * TOK:(2 * t + 1) * TOK, :] = x_in[:, cols]
        msg[(2 * t + 1) * TOK:(2 * t + 2) * TOK, :] = dy_in[:, cols]
    msg[META:MROWS, :] = meta_in[...]
    greet(me, core)
    own = pltpu.make_async_copy(msg, buf.at[index_of(me, core)], own_sem)
    own.start()

    def ring(r, pos, half, axis, d, mine=False):
        start, size = rows_of(SPLIT, r, half)
        idx = index_of(pos, core)
        src = msg if mine else buf.at[idx]
        return pltpu.make_async_remote_copy(
            src_ref=src.at[pl.ds(start, size)], dst_ref=buf.at[idx, pl.ds(start, size)],
            send_sem=send_sem, recv_sem=recv_sem.at[r, lin(pos), 0 if half is None else half],
            device_id=dev_of(moved(me, axis, d), core), device_id_type=MESH)

    def send_full(r, pos, phases, mine=False):
        for p in phases:
            for d in (1, -1):
                ring(r, pos, None, ORDER[r][p], d, mine).start()

    def forward(r, base, phase):
        axis = ORDER[r][phase]
        for d in (1, -1):
            ring(r, moved(base, axis, -d), 0 if d == 1 else 1, axis, d).start()

    def near(r, base, phase, later=(), onward=True):
        axis = ORDER[r][phase]
        for d in (1, -1):
            pos = moved(base, axis, -d)
            ring(r, pos, None, axis, d).wait_recv()
            if onward:
                ring(r, pos, 0 if d == 1 else 1, axis, d).start()
            send_full(r, pos, later)

    def far(r, base, phase, later=()):
        axis = ORDER[r][phase]
        pos = moved(base, axis, 2)
        for half in (0, 1):
            ring(r, pos, half, axis, 1).wait_recv()
        send_full(r, pos, later)

    def column(i):
        return moved(moved(me, 0, entry(COL_Z, i)), 1, entry(COL_X, i))

    def base_of(r, i):
        return moved(moved(me, 1 if r == 1 else 0, entry(NEAR4, i // 4)), 2, entry(NEAR4, i % 4))

    def issue(u):
        def whole():
            for r in (1, 2):
                send_full(r, base_of(r, u), (2,))

        def halves():
            for r in (1, 2):
                for k in range(2):
                    forward(r, base_of(r, 2 * (u - 16) + k), 2)
        if isinstance(u, int):
            whole()
        else:
            pl.when(u < 16)(whole)
            pl.when((u >= 16) & (u < 24))(halves)

    for r in range(3):
        send_full(r, me, (0, 1, 2), mine=True)
    gx[...] = jnp.zeros_like(gx)
    gd[...] = jnp.zeros_like(gd)
    for copy in weights_in:
        copy.wait()
    wx[:, :, 0:256] = wg[...]
    wx[:, :, 256:512] = wu[...]
    for j in range(2):
        wxt[j, 0:256] = wg[j].T
        wxt[j, 256:512] = wu[j].T
        wdt[j] = wd[j].T
    for r in range(3):
        near(r, me, 0, (1,))
    for r in range(3):
        far(r, me, 0, (1,))
    for i in (1,):
        send_full(0, column(i), (2,))

    def line(step):
        def body(i, c):
            for r in range(3):
                step(r, moved(me, ORDER[r][0], entry(NEAR4, i)), 1)
            return c
        return body
    lax.fori_loop(0, 4, line(near), 0)
    for u in (1, 2):
        issue(u)
    lax.fori_loop(0, 4, line(far), 0)

    own.wait()

    for u in range(3, LOOK):
        issue(u)
    def along_y(i):
        near(0, column(i), 2)

        @pl.when(i + AHEAD < 16)
        def _():
            send_full(0, column(i + AHEAD), (2,))

    def unit(u):
        @pl.when(u < 16)
        def _():
            for r in (1, 2):
                near(r, base_of(r, u), 2, onward=False)

        @pl.when((u >= 16) & (u < 24))
        def _():
            for r in (1, 2):
                for k in range(2):
                    far(r, base_of(r, 2 * (u - 16) + k), 2)
        issue(u + LOOK)

    def start_up(i, c):
        unit(i)
        pl.when(i < AHEAD - 1)(functools.partial(along_y, i))
        return c
    lax.fori_loop(0, 3, start_up, 0)

    slots = lax.broadcasted_iota(jnp.int32, (CAP, TOK), 0).astype(F32)

    def staged(k, at):
        return pltpu.make_async_copy(stage.at[pl.ds(k * 4, 4)], kept.at[pl.ds(pl.multiple_of(at * 4, 4), 4)], stage_sem.at[k])

    def send_rows(p, k):
        return pltpu.make_async_remote_copy(
            src_ref=away.at[k], dst_ref=rows.at[p % 2, 2 * k + core], send_sem=rows_send.at[k], recv_sem=rows_recv.at[k],
            device_id=other, device_id_type=MESH)

    def send_part(k):
        return pltpu.make_async_remote_copy(
            src_ref=part.at[2 * k + 1 - core], dst_ref=back.at[k], send_sem=part_send.at[k], recv_sem=part_recv.at[k],
            device_id=other, device_id_type=MESH)

    def pick(p, k):
        half = p % 2
        at = half * 8 + k * 4
        hots, gates = [[] for _ in range(4)], [0.0] * 4
        for y in range(4):
            meta = slab[at + y, pl.ds(META, 32), :].astype(F32)
            for j in range(4):
                named = (meta[0:8] == (firsts[j // 2] + j % 2).astype(F32)).astype(F32)
                where = jnp.sum(named * (meta[8:16] + 1.0), axis=0, keepdims=True) - 1.0
                gate = jnp.sum(named * (meta[16:24] + meta[24:32]), axis=0, keepdims=True)
                hot = (slots == where).astype(F32)
                hots[j].append(hot)
                gates[j] = gates[j] + hot * gate
        hot = jnp.concatenate([jnp.concatenate(h, axis=1) for h in hots], axis=0)
        gate = jnp.sum(jnp.concatenate(gates, axis=0), axis=1, keepdims=True)
        ps[k] = hot.T.astype(BF16)
        hot = hot.astype(BF16)
        for t in range(0, TILES, 2):
            for a in range(2):
                cols = jnp.concatenate([
                    jnp.concatenate([slab[at + y, pl.ds((t + u) * 2 * TOK + a * TOK, TOK), :] for u in range(2)], axis=1)
                    for y in range(4)], axis=0)
                got = jnp.dot(hot, cols, preferred_element_type=F32)
                got = (gate * got if a else got).astype(BF16)
                for j in range(2):
                    rows[half, 2 * k + core, a, j, :, pl.ds(t * LANES, 2 * LANES)] = got[j * CAP:(j + 1) * CAP]
                    away[k, a, j, :, pl.ds(t * LANES, 2 * LANES)] = got[(2 + j) * CAP:(3 + j) * CAP]

    def main(p, j):
        half = p % 2
        x = rows[half, :, 0, j].reshape(BLOCKS * CAP, 1024)
        s = rows[half, :, 1, j].reshape(BLOCKS * CAP, 1024)
        pre = jnp.dot(x, wx[j], preferred_element_type=F32)
        pre_gate, pre_up = pre[:, 0:256], pre[:, 256:512]
        d_hidden = jnp.dot(s, wdt[j], preferred_element_type=F32)
        sig = jax.nn.sigmoid(pre_gate)
        act = pre_gate * sig
        hidden = (act * pre_up).astype(BF16)
        d_up = (d_hidden * act).astype(BF16)
        d_gate = (d_hidden * pre_up * sig * (1.0 + pre_gate * (1.0 - sig))).astype(BF16)
        acts[j, :, 0:256] = hidden
        both = jnp.concatenate([d_gate, d_up], axis=1)
        acts[j, :, 256:768] = both
        part[:, j] = jnp.dot(both, wxt[j], preferred_element_type=F32).astype(BF16).reshape(BLOCKS, CAP, 1024)

    def weights(p, j):
        half = p % 2
        x = rows[half, :, 0, j].reshape(BLOCKS * CAP, 1024)
        s = rows[half, :, 1, j].reshape(BLOCKS * CAP, 1024)
        gd[j] += tn(acts[j, :, 0:256], s)
        gx[j] += tn(x, acts[j, :, 256:768])

    def place(k):
        hot = ps[k]
        for t in range(0, TILES, 2):
            cols = pl.ds(t * LANES, 2 * LANES)
            every = jnp.concatenate([part[2 * k + core, j, :, cols] for j in range(2)]
                                    + [back[k, j, :, cols] for j in range(2)], axis=0)
            out = jnp.dot(hot, every, preferred_element_type=F32).astype(BF16)
            for y in range(4):
                for u in range(2):
                    stage[k * 4 + y, pl.ds((t + u) * TOK, TOK), :] = out[y * TOK:(y + 1) * TOK, u * LANES:(u + 1) * LANES]

    def column_at(i):
        pos = column(i)
        return pos[0] * 4 + pos[1]

    def load(p, k):
        at = pl.multiple_of(column_at(2 * p + k) * 8 + core * 4, 4)
        half = p % 2
        return pltpu.make_async_copy(buf.at[pl.ds(at, 4)], slab.at[pl.ds(pl.multiple_of(half * 8 + k * 4, 4), 4)],
                                     load_sem.at[half, k])

    def compute(p, c):
        live, ready = p < 8, (p >= 1) & (p < 9)
        u = jnp.where(p < 5, 3 * p + 3, 2 * p + 8)
        unit(u)

        def picked(k):
            load(p - 1, k).wait()

            @pl.when(p >= 2)
            def _():
                send_rows(p, k).wait_send()
            pick(p - 1, k)
            send_rows(p - 1, k).start()
        pl.when(ready)(functools.partial(picked, 0))

        @pl.when(2 * p + AHEAD - 1 < 16)
        def _():
            along_y(2 * p + AHEAD - 1)
        unit(u + 1)
        pl.when(ready)(functools.partial(picked, 1))

        @pl.when(p >= 2)
        def _():
            for j in range(2):
                weights(p - 2, j)

        @pl.when(2 * p + AHEAD < 16)
        def _():
            along_y(2 * p + AHEAD)

        @pl.when(ready)
        def _():
            for k in range(2):
                send_rows(p - 1, k).wait_recv()

            @pl.when(p >= 2)
            def _():
                for k in range(2):
                    send_part(k).wait_send()
            for j in range(2):
                main(p - 1, j)
            for k in range(2):
                send_part(k).start()
        pl.when(p < 5)(lambda: unit(u + 2))

        @pl.when(live)
        def _():
            for k in range(2):
                far(0, column(2 * p + k), 2)
                load(p, k).start()

        @pl.when(ready)
        def _():
            @pl.when(p >= 2)
            def _():
                for k in range(2):
                    staged(k, 0).wait()
            for k in range(2):
                send_part(k).wait_recv()
                place(k)
                staged(k, column_at(2 * (p - 1) + k)).start()
        return c

    lax.fori_loop(0, 10, compute, 0)
    for k in range(2):
        staged(k, 0).wait()
        send_rows(0, k).wait_send()
        send_part(k).wait_send()
    most = buf.at[pl.ds(0, 63)]
    pltpu.make_async_copy(most, most, send_sem).wait()


def gather_and_compute(x, dy, meta, wg, wu, wd):
    dma = pltpu.SemaphoreType.DMA
    hbm, vmem = pl.BlockSpec(memory_space=pl.ANY), pl.BlockSpec(memory_space=pltpu.VMEM)
    g = jax.ShapeDtypeStruct((2, 1024, 512), F32)
    d = jax.ShapeDtypeStruct(wd.shape, F32)
    bf = lambda *shape: pltpu.VMEM(shape, BF16)
    return pl.pallas_call(
        gather_kernel,
        out_shape=(jax.ShapeDtypeStruct((128, MROWS, LANES), BF16),
                   jax.ShapeDtypeStruct((64, TILES * TOK, LANES), BF16), g, d),
        in_specs=[vmem] * 3 + [hbm] * 3,
        out_specs=(hbm, hbm, vmem, vmem),
        scratch_shapes=[bf(16, MROWS, LANES), bf(2, BLOCKS, 2, 2, CAP, 1024), bf(2, 2, 2, CAP, 1024), bf(2, 512, 4 * CAP),
                        bf(BLOCKS, 2, CAP, 1024), bf(2, 2, CAP, 1024), bf(2, BLOCKS * CAP, 768), bf(8, TILES * TOK, LANES), bf(2, 1024, 512), bf(2, 512, 1024), bf(2, 1024, 256), bf(MROWS, LANES),
                        bf(2, 1024, 256), bf(2, 1024, 256), bf(2, 256, 1024), dma((3,)),
                        dma, dma((3, 64, 2)), dma, dma((2, 2)), dma((2,)), dma((2,)), dma((2,)), dma((2,)), dma((2,))],
        compiler_params=pltpu.CompilerParams(collective_id=0, has_side_effects=True, vmem_limit_bytes=60 * 1024 * 1024),
    )(x, dy, meta, wg, wu, wd)


OFFSETS = ((2,), (1, -1), (0,))
EARLY = 4
LAG = 2
FAR4 = (2, 1, 3, 0)


def scatter_kernel(kept, out, mine, land, send_sem, recv_sem, load_sem, out_sem):
    me, core = where_am_i()
    greet(me, core)

    def slot(r, pos, phase):
        a = [pos[k] for k in ORDER[r]]
        return (20, 16 + a[0], a[0] * 4 + a[1])[phase]

    def hop(r, pos, phase, kind, d):
        half = None if kind else (0 if d == 1 else 1)
        start, size = rows_of(BACK, r, half)
        s = slot(r, pos, phase)
        lane = 2 if kind == 0 else (0 if d == 1 else 1)
        sem = (0 if d == 1 else 1) + 2 * kind
        return pltpu.make_async_remote_copy(
            src_ref=mine.at[lin(pos), pl.ds(start, size)],
            dst_ref=land.at[r, s * 3 + lane, pl.ds(start - BACK[r][0], size)],
            send_sem=send_sem, recv_sem=recv_sem.at[r, s, sem],
            device_id=dev_of(moved(me, ORDER[r][phase], d), core), device_id_type=MESH)

    def add(r, pos, phase, kind, d):
        hop(r, pos, phase, kind, d).wait_recv()
        half = None if kind else (0 if d == 1 else 1)
        start, size = rows_of(BACK, r, half)
        lane = 2 if kind == 0 else (0 if d == 1 else 1)
        rows = pl.ds(start, size)
        mine[lin(pos), rows, :] = (mine[lin(pos), rows, :]
                                   + land[r, slot(r, pos, phase) * 3 + lane, pl.ds(start - BACK[r][0], size), :])

    def far(r, base, phase):
        pos = moved(base, ORDER[r][phase], 2)
        for d in (1, -1):
            hop(r, pos, phase, 0, d).start()

    def near(r, base, phase):
        for d in (1, -1):
            pos = moved(base, ORDER[r][phase], d)
            add(r, pos, phase, 0, d)
            hop(r, pos, phase, 1, d).start()

    def here(r, base, phase):
        for d in (1, -1):
            add(r, base, phase, 1, d)

    def plane_base(r, i):
        return moved(moved(me, ORDER[r][0], entry(FAR4, i // 4)), ORDER[r][1], entry(FAR4, i % 4))

    def lines(step, l):
        for r in range(3):
            step(r, moved(me, ORDER[r][0], entry(FAR4, l)), 1)

    def ends(step):
        for r in range(3):
            step(r, me, 0)

    def fetch(kind, i):
        for r in range(3):
            start, size = BACK[r]
            for o in OFFSETS[kind]:
                pos = moved(plane_base(r, i), ORDER[r][2], o)
                pltpu.make_async_copy(kept.at[lin(pos), pl.ds(start, size)], mine.at[lin(pos), pl.ds(start, size)],
                                      load_sem.at[kind, i]).start()

    for kind in range(3):
        for i in range(EARLY - kind * LAG):
            fetch(kind, i)

    def plane(i, c):
        for kind, step in enumerate((far, near, here)):
            k = i - kind * LAG

            @pl.when((k + EARLY < 16) & (k + EARLY >= 0))
            def _(kind=kind, k=k):
                fetch(kind, k + EARLY)
        for kind, step in enumerate((far, near, here)):
            k = i - kind * LAG

            @pl.when((k >= 0) & (k < 16))
            def _(kind=kind, k=k, step=step):
                n = len(OFFSETS[kind])
                pltpu.make_async_copy(mine.at[pl.ds(0, n)], mine.at[pl.ds(0, n)], load_sem.at[kind, k]).wait()
                for r in range(3):
                    step(r, plane_base(r, k), 2)
        k = i - 2 * LAG
        for l in range(4):
            @pl.when(k == 4 * l + 3)
            def _(l=l):
                lines(far, l)
                if l >= 1:
                    lines(near, l - 1)
                if l >= 2:
                    lines(here, l - 2)
                if l == 2:
                    ends(far)
        return c
    lax.fori_loop(0, 16 + 2 * LAG, plane, 0)
    lines(here, 2)
    ends(near)
    lines(near, 3)
    lines(here, 3)
    ends(here)
    done = pltpu.make_async_copy(mine.at[lin(me)], out, out_sem)
    done.start()
    done.wait()
    most = mine.at[pl.ds(0, 63)]
    pltpu.make_async_copy(most, most, send_sem).wait()


def scatter_all(kept):
    dma = pltpu.SemaphoreType.DMA
    rows = TILES * TOK
    return pl.pallas_call(
        scatter_kernel,
        out_shape=jax.ShapeDtypeStruct((rows, LANES), BF16),
        in_specs=[pl.BlockSpec(memory_space=pl.ANY)],
        out_specs=pl.BlockSpec(memory_space=pl.ANY),
        scratch_shapes=[pltpu.VMEM((64, rows, LANES), BF16),
                        pltpu.VMEM((3, 63, 352, LANES), BF16),
                        dma, dma((3, 21, 4)), dma((3, 16)), dma],
        compiler_params=pltpu.CompilerParams(collective_id=1, has_side_effects=True, vmem_limit_bytes=60 * 1024 * 1024),
    )(kept)


PIECES = 2


def write_kernel(both, down, back, tokens_out, gate_out, up_out, down_out):
    @pl.when(pl.program_id(0) == 0)
    def _():
        for t in range(TILES):
            tokens_out[:, t * LANES:(t + 1) * LANES] = back[t * TOK:(t + 1) * TOK, :]
    gate_out[...] = both[:, :, 0:256]
    up_out[...] = both[:, :, 256:512]
    down_out[...] = down[...]


def write_all(both, down, back):
    piece = lambda r, c: pl.BlockSpec((1, r // PIECES, c), lambda i: (i // PIECES, i % PIECES, 0))
    whole = lambda *shape: pl.BlockSpec(shape, lambda i: (0, 0))
    return pl.pallas_call(
        write_kernel,
        grid=(2 * PIECES,),
        out_shape=(jax.ShapeDtypeStruct((TOK, TILES * LANES), BF16), jax.ShapeDtypeStruct((2, 1024, 256), F32),
                   jax.ShapeDtypeStruct((2, 1024, 256), F32), jax.ShapeDtypeStruct((2, 256, 1024), F32)),
        in_specs=[piece(1024, 512), piece(256, 1024), whole(TILES * TOK, LANES)],
        out_specs=(whole(TOK, TILES * LANES), piece(1024, 256), piece(1024, 256), piece(256, 1024)),
        compiler_params=pltpu.CompilerParams(vmem_limit_bytes=32 * 1024 * 1024),
    )(both, down, back)


def shards(tokens, out_grad, routes, gates, w_gate, w_up, w_down):
    y = lax.axis_index("mp")
    ids = jnp.arange(64, dtype=jnp.int32)
    named = jnp.sum((routes[:, :, None] == ids).astype(F32), axis=1)
    below = jnp.tril(jnp.ones((512, 512), F32), -1)
    before = jnp.dot(below.astype(BF16), named.astype(BF16), preferred_element_type=F32)
    before = jnp.sum(jnp.where(routes[:, :, None] == ids, before[:, None, :], 0.0), axis=2)
    own = lambda a: lax.dynamic_slice_in_dim(a, y * TOK, TOK, axis=0).T
    gate = own(gates)
    high = lax.reduce_precision(gate, 8, 7)
    meta = jnp.concatenate([own(routes).astype(F32), own(before), high, gate - high], axis=0).astype(BF16)
    _, kept, both, grad_down = gather_and_compute(tokens, out_grad, meta, w_gate, w_up, w_down)
    return write_all(both, grad_down, scatter_all(kept))


def solution(mesh):
    in_specs = (
        P(("expert", "mp"), None),
        P(("expert", "mp"), None),
        P("expert", None),
        P("expert", None),
        P("expert", None, "mp"),
        P("expert", None, "mp"),
        P("expert", "mp", None),
    )
    out_specs = (
        P(("expert", "mp"), None),
        P("expert", None, "mp"),
        P("expert", None, "mp"),
        P("expert", "mp", None),
    )
    return jax.shard_map(shards, mesh=mesh, in_specs=in_specs, out_specs=out_specs, check_vma=False)
```
